128 devices in a mesh: row: 4 (over x), col: 2 (over core), depth: 16 (over z, y).
Axes of the slice: x: 4, y: 4, z: 4, core: 2. Of those that a mesh axis runs over, the one named last changes fastest.
Arguments:
- tokens: bfloat16 [4096, 3072], P(('col', 'depth'), 'row'), may hold values from -6 to 6
- up_weight: bfloat16 [3072, 12288], P('row', ('col', 'depth')), may hold values from -0.109375 to 0.109375
- down_weight: bfloat16 [12288, 3072], P(('col', 'depth'), 'row'), may hold values from -0.0546875 to 0.0546875
- out_grad: bfloat16 [4096, 3072], P(('col', 'depth'), 'row'), may hold values from -6 to 6
Outputs:
- mixed: bfloat16 [4096, 3072], P(('col', 'depth'), 'row')
- input_grad: bfloat16 [4096, 3072], P(('col', 'depth'), 'row')
- up_grad: float32 [3072, 12288], P('row', ('col', 'depth'))
- down_grad: float32 [12288, 3072], P(('col', 'depth'), 'row')
The draws below stay inside these ranges and needn't reach their ends.
All inputs are finite; a program needn't handle non-finite values.
Results may differ from the reference program's by a relative error of at most 0.029.
Values may be sent and summed in bfloat16 or wider, within the bound.
No kernel may reach another device: no remote copies, remote signals or barrier semaphores. Data moves between devices by JAX's collectives and lax.ppermute only.
A program may use at most 128 MiB of HBM per device.

```python
import jax
import jax.numpy as jnp
from jax import lax

D = 3072
FF = 12288
TOKENS = 4096
N_ROW = 4
N_COL = 2
N_DEPTH = 16


def level_of(rng, extent, shards, low, high):
    loudness = 1.0
    for axis_at, blocks in shards:
        steps = jax.random.uniform(jax.random.fold_in(jax.random.fold_in(rng, 6), axis_at), (blocks,), jnp.float32, low / len(shards), high / len(shards))
        loudness = loudness * jnp.repeat(jnp.exp(steps), extent[axis_at] // blocks).reshape((-1,) + (1,) * (len(extent) - 1 - axis_at))
    return loudness


def centred(own_key, shape, width, bound, shards=(), held_as=jnp.bfloat16):
    array = jax.random.normal(own_key, shape, jnp.float32) * width
    if len(shards) > 0:
        array = level_of(own_key, shape, shards, -0.22, 0.18) * array
    return jnp.clip(array, min=-bound, max=bound).astype(held_as)


def setup_inputs(seed: int = 0) -> dict:
    arg_keys = jax.random.split(jax.random.key(seed), 5)
    return {
        "tokens": centred(arg_keys[0], (TOKENS, D), 1.0, 6.0, ((0, 32), (1, 4))),
        "up_weight": centred(arg_keys[1], (D, FF), D ** -0.5, 0.109375, ((0, 4), (1, 32))),
        "down_weight": centred(arg_keys[2], (FF, D), FF ** -0.5, 0.0546875, ((0, 32), (1, 4))),
        "out_grad": centred(arg_keys[3], (TOKENS, D), 1.0, 6.0, ((0, 32), (1, 4))),
    }


def block_sum(left_blocks, right_blocks):
    def step(total, pair):
        product = jnp.dot(pair[0], pair[1], preferred_element_type=jnp.float32)
        rounded = lax.optimization_barrier(product.astype(jnp.bfloat16))
        return total + rounded.astype(jnp.float32), None
    init = jnp.zeros((left_blocks.shape[1], right_blocks.shape[2]), jnp.float32)
    total, unused = lax.scan(step, init, (left_blocks, right_blocks))
    return total


def split_columns(matrix, pieces):
    return matrix.reshape(matrix.shape[0], pieces, matrix.shape[1] // pieces).transpose(1, 0, 2)


def split_rows(matrix, pieces):
    return matrix.reshape(pieces, matrix.shape[0] // pieces, matrix.shape[1])


def gelu_value(value):
    return value * 0.5 * (1.0 + lax.erf(value * 0.7071067811865476))


def gelu_slope(value):
    return 0.5 * (1.0 + lax.erf(value * 0.7071067811865476)) + value * jnp.exp(-0.5 * value * value) * 0.3989422804014327


def reference(tokens, up_weight, down_weight, out_grad):
    groups = N_COL * N_DEPTH
    hidden = block_sum(split_columns(tokens, N_ROW), split_rows(up_weight, N_ROW))
    activated = gelu_value(hidden).astype(jnp.bfloat16)
    mixed = block_sum(split_columns(activated, groups), split_rows(down_weight, groups)).astype(jnp.bfloat16)
    act_grad = block_sum(split_columns(out_grad, N_ROW), split_rows(down_weight.T, N_ROW))
    hidden_grad = (act_grad * gelu_slope(hidden)).astype(jnp.bfloat16)
    input_grad = block_sum(split_columns(hidden_grad, groups), split_rows(up_weight.T, groups)).astype(jnp.bfloat16)
    up_grad = jnp.dot(tokens.T, hidden_grad, preferred_element_type=jnp.float32)
    down_grad = jnp.dot(activated.T, out_grad, preferred_element_type=jnp.float32)
    return mixed, input_grad, up_grad, down_grad
```

```python
import jax
import jax.numpy as jnp
from jax import lax
from jax.sharding import PartitionSpec as P

BF = jnp.bfloat16
F32 = jnp.float32


def gelu_value(value):
    return value * 0.5 * (1.0 + lax.erf(value * 0.7071067811865476))


def gelu_slope(value):
    return (
        0.5 * (1.0 + lax.erf(value * 0.7071067811865476))
        + value * jnp.exp(-0.5 * value * value) * 0.3989422804014327
    )


def product(left, right, left_dim, right_dim):
    return lax.dot_general(
        left, right, (((left_dim,), (right_dim,)), ((), ())), preferred_element_type=F32
    )


def along_x(value, hop):
    return lax.ppermute(value, "row", [(i, (i + hop) % 4) for i in range(4)])


def across(value):
    return lax.ppermute(value, "col", [(0, 1), (1, 0)])


def plane(value, phase, hop):
    pairs = []
    for core in range(2):
        for z in range(4):
            for y in range(4):
                if core == phase:
                    to = ((z + hop) % 4) * 4 + y
                else:
                    to = z * 4 + (y + hop) % 4
                pairs.append((core * 16 + z * 4 + y, core * 16 + to))
    return lax.ppermute(value, ("col", "depth"), pairs)


def on_device(tokens, up_weight, down_weight, out_grad):
    x = lax.axis_index("row")
    rows, width = tokens.shape
    sub = rows // 4
    hid = up_weight.shape[1]

    def gather_weight(weight, axis):
        parts = [weight] + [along_x(weight, hop) for hop in (1, 2, 3)]
        mine = jnp.concatenate(parts, axis=axis)
        return jnp.concatenate([mine, across(mine)], axis=1 - axis)

    both = jnp.stack([tokens, out_grad]).reshape(2, 4, sub, width)

    def piece(k):
        return lax.dynamic_index_in_dim(both, (x + k) % 4, 1, keepdims=False)

    parts = [piece(0)] + [along_x(piece(k), k) for k in (1, 2, 3)]
    own = jnp.concatenate(parts, axis=2)
    first = [own] + [plane(own, 0, hop) for hop in (1, 2, 3)]
    first = jnp.concatenate(first, axis=1)

    def second(value):
        return jnp.concatenate([value] + [plane(value, 1, hop) for hop in (1, 2, 3)], axis=0)

    feats = second(first[0])
    up = gather_weight(up_weight, 0)
    cots = second(first[1])
    down = gather_weight(down_weight, 1)

    hidden = product(feats, up, 1, 0)
    activated = gelu_value(hidden).astype(BF)
    act_grad = product(cots, down, 1, 1)
    hidden_grad = (act_grad * gelu_slope(hidden)).astype(BF)

    def scatter(value):
        value = value.reshape(4, rows, 4 * width)
        total = value[0].astype(F32)
        for hop in (1, 2, 3):
            total = total + plane(value[hop].astype(BF), 1, -hop).astype(F32)
        total = total.reshape(4, sub, 4 * width)
        end = total[0]
        for hop in (1, 2, 3):
            end = end + plane(total[hop].astype(BF), 0, -hop).astype(F32)
        end = end.astype(BF).reshape(sub, 4, width)
        pieces = [end[:, 0]] + [along_x(end[:, k], -k) for k in (1, 2, 3)]
        return jnp.roll(jnp.concatenate(pieces, axis=0), x * sub, axis=0)

    mixed = scatter(product(activated, down, 1, 0))
    input_grad = scatter(product(hidden_grad, up, 1, 1))

    def reduce_weight(partial, axis):
        mine = lax.slice_in_dim(partial, 0, hid, axis=1 - axis)
        other = lax.slice_in_dim(partial, hid, 2 * hid, axis=1 - axis)
        total = mine + across(other.astype(BF)).astype(F32)

        def block(k):
            return lax.slice_in_dim(total, k * width, (k + 1) * width, axis=axis)

        end = block(0)
        for k in (1, 2, 3):
            end = end + along_x(block(k).astype(BF), -k).astype(F32)
        return end

    down_grad = reduce_weight(product(activated, cots, 0, 0), 1)
    up_grad = reduce_weight(product(feats, hidden_grad, 0, 0), 0)
    return mixed, input_grad, up_grad, down_grad


def solution(mesh):
    spec = P(("col", "depth"), "row")
    wide = P("row", ("col", "depth"))
    return jax.shard_map(
        on_device,
        mesh=mesh,
        in_specs=(spec, wide, spec, spec),
        out_specs=(spec, spec, wide, spec),
        check_vma=False,
    )
```

```python
import jax
import jax.numpy as jnp
from jax import lax
from jax.sharding import PartitionSpec as P

BF = jnp.bfloat16
F32 = jnp.float32


def gelu_value(value):
    return value * 0.5 * (1.0 + lax.erf(value * 0.7071067811865476))


def gelu_slope(value):
    return (
        0.5 * (1.0 + lax.erf(value * 0.7071067811865476))
        + value * jnp.exp(-0.5 * value * value) * 0.3989422804014327
    )


def product(left, right, left_dim, right_dim):
    return lax.dot_general(
        left, right, (((left_dim,), (right_dim,)), ((), ())), preferred_element_type=F32
    )


def along_x(value, hop):
    pairs = []
    for row in range(4):
        for core in range(2):
            to = (row + (hop if core == 0 else -hop)) % 4
            pairs.append((row * 2 + core, to * 2 + core))
    return lax.ppermute(value, ("row", "col"), pairs)


def across(value):
    return lax.ppermute(value, "col", [(0, 1), (1, 0)])


def plane(value, phase, hop):
    pairs = []
    for core in range(2):
        for z in range(4):
            for y in range(4):
                if core == phase:
                    to = ((z + hop) % 4) * 4 + y
                else:
                    to = z * 4 + (y + hop) % 4
                pairs.append((core * 16 + z * 4 + y, core * 16 + to))
    return lax.ppermute(value, ("col", "depth"), pairs)


def on_device(tokens, up_weight, down_weight, out_grad):
    x = lax.axis_index("row")
    sign = 1 - 2 * lax.axis_index("col")
    rows, width = tokens.shape
    sub = rows // 4
    hid = up_weight.shape[1]

    both = jnp.stack([tokens, out_grad]).reshape(2, 4, sub, width)

    def piece(k):
        return lax.dynamic_index_in_dim(both, (x + sign * k + 4) % 4, 1, keepdims=False)

    own = jnp.concatenate([piece(0)] + [along_x(piece(k), k) for k in (1, 2, 3)], axis=2)

    def gather_weight(mine, axis):
        early = across(jnp.concatenate(mine[:3], axis=axis))
        late = across(mine[3])
        early = [lax.slice_in_dim(early, k * width, (k + 1) * width, axis=axis) for k in range(3)]
        theirs = [early[0], late, early[2], early[1]]
        blocks = [jnp.concatenate(pair, axis=1 - axis) for pair in zip(mine, theirs)]
        return jnp.concatenate(blocks, axis=axis)

    ups, downs = [up_weight], [down_weight]
    ups.append(along_x(ups[-1], 1))
    own, ups[-1] = lax.optimization_barrier((own, ups[-1]))

    ups.append(along_x(ups[-1], 1))
    downs.append(along_x(downs[-1], 1))
    first = [own] + [plane(own, 0, hop) for hop in (1, 2, 3)]
    first = jnp.concatenate(first, axis=1)
    first, ups[-1], downs[-1] = lax.optimization_barrier((first, ups[-1], downs[-1]))

    ups.append(along_x(ups[-1], 1))
    downs.append(along_x(downs[-1], 1))
    tok, cot = [first[0]], [first[1]]
    tok.append(plane(tok[-1], 1, 1))
    cot.append(plane(cot[-1], 1, -1))
    tok[-1], cot[-1], ups[-1], downs[-1] = lax.optimization_barrier(
        (tok[-1], cot[-1], ups[-1], downs[-1])
    )

    downs.append(along_x(downs[-1], 1))
    up = gather_weight(ups, 0)
    tok.append(plane(tok[-1], 1, 1))
    cot.append(plane(cot[-1], 1, -1))
    tok[-1], cot[-1], downs[-1] = lax.optimization_barrier((tok[-1], cot[-1], downs[-1]))

    down = gather_weight(downs, 1)
    tok.append(plane(tok[-1], 1, 1))
    cot.append(plane(cot[-1], 1, -1))
    cot = [cot[0], cot[3], cot[2], cot[1]]

    hidden = [product(part, up, 1, 0) for part in tok]
    activated = [gelu_value(part).astype(BF) for part in hidden]
    act_grad = [product(part, down, 1, 1) for part in cot]
    hidden_grad = [(a * gelu_slope(h)).astype(BF) for a, h in zip(act_grad, hidden)]

    acts, hgs = jnp.concatenate(activated, axis=0), jnp.concatenate(hidden_grad, axis=0)
    feats, cots = jnp.concatenate(tok, axis=0), jnp.concatenate(cot, axis=0)

    def block(value, k):
        return lax.slice_in_dim(value, k * width, (k + 1) * width, axis=1)

    def mixed_part(j):
        return product(activated[j], down, 1, 0)

    def back_part(j):
        return product(hidden_grad[j], up, 1, 1)

    def down_part(k):
        part = product(acts[:, :hid], block(cots, k), 0, 0)
        return part + block(down_theirs, (4 - k) % 4).astype(F32)

    def up_part(k):
        at = ((4 - k) % 4) * width
        part = product(block(feats, k), hgs[:, :hid], 0, 0)
        return part + lax.slice_in_dim(up_theirs, at, at + width, axis=0).astype(F32)

    def both_steps(mixed, back, j_mixed, j_back, *others):
        mixed, back = plane(mixed, 1, 1), plane(back, 1, -1)
        mixed, back, *others = lax.optimization_barrier((mixed, back) + others)
        mixed = (mixed.astype(F32) + mixed_part(j_mixed)).astype(BF)
        back = (back.astype(F32) + back_part(j_back)).astype(BF)
        return mixed, back, *others

    mixed, back = mixed_part(1).astype(BF), back_part(3).astype(BF)
    down_theirs = across(product(acts[:, hid:], cots, 0, 0).astype(BF))
    mixed, back, down_theirs = both_steps(mixed, back, 2, 2, down_theirs)

    up_theirs = across(product(feats, hgs[:, hid:], 0, 0).astype(BF))
    down_grad = along_x(down_part(1).astype(BF), 1)
    mixed, back, up_theirs, down_grad = both_steps(mixed, back, 3, 1, up_theirs, down_grad)

    down_grad = along_x((down_grad.astype(F32) + down_part(2)).astype(BF), 1)
    up_grad = along_x(up_part(1).astype(BF), 1)
    mixed, back, down_grad, up_grad = both_steps(mixed, back, 0, 0, down_grad, up_grad)

    down_grad = along_x((down_grad.astype(F32) + down_part(3)).astype(BF), 1)
    up_grad = along_x((up_grad.astype(F32) + up_part(2)).astype(BF), 1)
    total = jnp.stack([mixed, back]).reshape(2, 4, sub, 4 * width)
    end = total[:, 0].astype(F32)
    for hop in (1, 2, 3):
        end = end + plane(total[:, hop], 0, -hop).astype(F32)
    end, down_grad, up_grad = lax.optimization_barrier((end.astype(BF), down_grad, up_grad))

    up_grad = along_x((up_grad.astype(F32) + up_part(3)).astype(BF), 1)
    end = end.reshape(2, sub, 4, width)
    pieces = [end[:, :, 0]] + [along_x(end[:, :, k], -k) for k in (1, 2, 3)]
    ordered = [lax.select_n(sign > 0, pieces[(4 - k) % 4], pieces[k]) for k in range(4)]
    out = jnp.roll(jnp.concatenate(ordered, axis=1), x * sub, axis=1)
    down_grad = down_grad.astype(F32) + down_part(0)
    up_grad = up_grad.astype(F32) + up_part(0)
    return out[0], out[1], up_grad, down_grad


def solution(mesh):
    spec = P(("col", "depth"), "row")
    wide = P("row", ("col", "depth"))
    return jax.shard_map(
        on_device,
        mesh=mesh,
        in_specs=(spec, wide, spec, spec),
        out_specs=(spec, spec, wide, spec),
        check_vma=False,
    )
```

```python
import jax
import jax.numpy as jnp
from jax import lax
from jax.experimental import pallas as pl
from jax.experimental.pallas import tpu as pltpu
from jax.sharding import PartitionSpec as P

BF = jnp.bfloat16
F32 = jnp.float32


def gelu_value(value):
    return value * 0.5 * (1.0 + lax.erf(value * 0.7071067811865476))


def gelu_slope(value):
    return (
        0.5 * (1.0 + lax.erf(value * 0.7071067811865476))
        + value * jnp.exp(-0.5 * value * value) * 0.3989422804014327
    )


def product(left, right, left_dim, right_dim):
    return lax.dot_general(
        left, right, (((left_dim,), (right_dim,)), ((), ())), preferred_element_type=F32
    )


def along_x(value, hop):
    pairs = []
    for row in range(4):
        for core in range(2):
            to = (row + (hop if core == 0 else -hop)) % 4
            pairs.append((row * 2 + core, to * 2 + core))
    return lax.ppermute(value, ("row", "col"), pairs)


def across(value):
    return lax.ppermute(value, "col", [(0, 1), (1, 0)])


def plane(value, phase, hop):
    pairs = []
    for core in range(2):
        for z in range(4):
            for y in range(4):
                if core == phase:
                    to = ((z + hop) % 4) * 4 + y
                else:
                    to = z * 4 + (y + hop) % 4
                pairs.append((core * 16 + z * 4 + y, core * 16 + to))
    return lax.ppermute(value, ("col", "depth"), pairs)


def held(*values):
    return lax.optimization_barrier(values)


def assemble(kernel_copies, shape, *arrays):
    def kernel(*refs):
        arrays, out, sems = refs[:-2], refs[-2], refs[-1]
        copies = [
            pltpu.make_async_copy(source, target, sems.at[at])
            for at, (source, target) in enumerate(kernel_copies(arrays, out))
        ]
        for copy in copies:
            copy.start()
        for copy in copies:
            copy.wait()

    return pl.pallas_call(
        kernel,
        out_shape=jax.ShapeDtypeStruct(shape, BF),
        in_specs=[pl.BlockSpec(memory_space=pl.ANY)] * len(arrays),
        out_specs=pl.BlockSpec(memory_space=pl.ANY),
        scratch_shapes=[pltpu.SemaphoreType.DMA((8,))],
        cost_estimate=pl.CostEstimate(
            flops=0, bytes_accessed=4 * shape[0] * shape[1], transcendentals=0
        ),
    )(*arrays)


def on_device(tokens, up_weight, down_weight, out_grad):
    rows, width = tokens.shape
    sub, half = rows // 4, rows // 2
    hid = up_weight.shape[1]

    def block_of(k):
        sign = 1 - 2 * lax.axis_index("col")
        return (lax.axis_index("row") - sign * k + 4) % 4

    both = jnp.stack([tokens, out_grad]).reshape(2, 4, sub, width).transpose(1, 0, 2, 3)
    own = lax.all_to_all(both, "row", 0, 0, tiled=True)
    own = own.transpose(1, 2, 0, 3).reshape(2, sub, 4 * width)

    downs = lax.all_gather(down_weight, "row", axis=0, tiled=False)
    ups = [up_weight, along_x(up_weight, 1)]
    first = jnp.concatenate([own] + [plane(own, 0, hop) for hop in (1, 2, 3)], axis=1)
    first, ups[1] = held(first, ups[1])
    tok, cot = [first[0]], [first[1]]

    ups.append(along_x(ups[1], 1))
    tok_left, tok_right = plane(tok[0], 1, 1), plane(tok[0], 1, -1)
    cot_left, cot_right = plane(cot[0], 1, 1), plane(cot[0], 1, -1)
    tok_left, tok_right, cot_left, cot_right, ups[2] = held(
        tok_left, tok_right, cot_left, cot_right, ups[2]
    )

    ups.append(along_x(ups[2], 1))
    early = across(jnp.concatenate(ups[:3], axis=0))
    late = across(ups[3])
    tok_far = [plane(tok_left[:half], 1, 1), plane(tok_right[half:], 1, -1)]
    cot_far = [plane(cot_left[:half], 1, 1), plane(cot_right[half:], 1, -1)]
    tok += [tok_left, jnp.concatenate(tok_far, axis=0), tok_right]
    cot += [cot_left, jnp.concatenate(cot_far, axis=0), cot_right]

    def up_copies(refs, out):
        *mine, early, late = refs
        copies = []
        for k in range(4):
            at = pl.ds(pl.multiple_of(block_of(k) * width, width), width)
            copies.append((mine[k], out.at[at, pl.ds(0, hid)]))
            at = pl.ds(pl.multiple_of(block_of(4 - k) * width, width), width)
            source = early.at[pl.ds(k * width, width)] if k < 3 else late
            copies.append((source, out.at[at, pl.ds(hid, hid)]))
        return copies

    def down_copies(refs, out):
        return [
            (refs[core].at[k], out.at[pl.ds(core * hid, hid), pl.ds(k * width, width)])
            for core in range(2)
            for k in range(4)
        ]

    up = assemble(up_copies, (4 * width, 2 * hid), *ups, early, late)
    down = assemble(down_copies, (2 * hid, 4 * width), downs, across(downs))

    hidden = [product(part, up, 1, 0) for part in tok]
    activated = [gelu_value(part).astype(BF) for part in hidden]
    act_grad = [product(part, down, 1, 1) for part in cot]
    hidden_grad = [(a * gelu_slope(h)).astype(BF) for a, h in zip(act_grad, hidden)]

    acts, hgs = jnp.concatenate(activated, axis=0), jnp.concatenate(hidden_grad, axis=0)
    feats, cots = jnp.concatenate(tok, axis=0), jnp.concatenate(cot, axis=0)

    def mixed_part(j):
        return product(activated[j], down, 1, 0)

    def back_part(j):
        return product(hidden_grad[j], up, 1, 1)

    def send_far(part):
        part = part.astype(BF)
        return [plane(part[:half], 1, -1), plane(part[half:], 1, 1)]

    def send_near(part, far, side):
        far = far.astype(F32)
        if side == 0:
            sent = jnp.concatenate([part[:half] + far, part[half:]], axis=0)
        else:
            sent = jnp.concatenate([part[:half], part[half:] + far], axis=0)
        return plane(sent.astype(BF), 1, -1 if side == 0 else 1)

    mixed_far = send_far(mixed_part(2))
    down_theirs = across(product(acts[:, hid:], cots, 0, 0).astype(BF))
    back_far = send_far(back_part(2))
    down_sum = (product(acts[:, :hid], cots, 0, 0) + down_theirs.astype(F32)).astype(BF)
    down_sum = down_sum.reshape(hid, 4, width).transpose(1, 0, 2)
    down_grad = lax.psum_scatter(down_sum, "row", scatter_dimension=0, tiled=False).astype(F32)

    up_theirs = across(product(feats, hgs[:, hid:], 0, 0).astype(BF))
    mixed_near = [send_near(mixed_part(1), mixed_far[0], 0), send_near(mixed_part(3), mixed_far[1], 1)]
    back_near = [send_near(back_part(1), back_far[0], 0), send_near(back_part(3), back_far[1], 1)]

    def up_part(k):
        at = block_of(k) * width
        part = product(
            lax.dynamic_slice_in_dim(feats, at, width, axis=1), hgs[:, :hid], 0, 0
        )
        return part + lax.dynamic_slice_in_dim(up_theirs, at, width, axis=0).astype(F32)

    up_grad = along_x(up_part(1).astype(BF), 1)
    mixed = (mixed_part(0) + mixed_near[0].astype(F32) + mixed_near[1].astype(F32)).astype(BF)
    back = (back_part(0) + back_near[0].astype(F32) + back_near[1].astype(F32)).astype(BF)
    mixed, back, up_grad = held(mixed, back, up_grad)

    up_grad = along_x((up_grad.astype(F32) + up_part(2)).astype(BF), 1)
    total = jnp.stack([mixed, back]).reshape(2, 4, sub, 4 * width)
    end = total[:, 0].astype(F32)
    for hop in (1, 2, 3):
        end = end + plane(total[:, hop], 0, -hop).astype(F32)
    end, up_grad = held(end.astype(BF), up_grad)

    up_grad = along_x((up_grad.astype(F32) + up_part(3)).astype(BF), 1)
    end = end.reshape(2, sub, 4, width).transpose(2, 0, 1, 3)
    out = lax.all_to_all(end, "row", 0, 0, tiled=True)
    out = out.transpose(1, 0, 2, 3).reshape(2, rows, width)
    up_grad = up_grad.astype(F32) + up_part(0)
    return out[0], out[1], up_grad, down_grad


def solution(mesh):
    spec = P(("col", "depth"), "row")
    wide = P("row", ("col", "depth"))
    return jax.shard_map(
        on_device,
        mesh=mesh,
        in_specs=(spec, wide, spec, spec),
        out_specs=(spec, spec, wide, spec),
        check_vma=False,
    )
```

```python
import jax
import jax.numpy as jnp
from jax import lax
from jax.sharding import PartitionSpec as P

BF = jnp.bfloat16
F32 = jnp.float32


def gelu_value(value):
    return value * 0.5 * (1.0 + lax.erf(value * 0.7071067811865476))


def gelu_slope(value):
    return (
        0.5 * (1.0 + lax.erf(value * 0.7071067811865476))
        + value * jnp.exp(-0.5 * value * value) * 0.3989422804014327
    )


def product(left, right, left_dim, right_dim):
    return lax.dot_general(
        left, right, (((left_dim,), (right_dim,)), ((), ())), preferred_element_type=F32
    )


def along_x(value, hop):
    pairs = []
    for row in range(4):
        for core in range(2):
            to = (row + (hop if core == 0 else -hop)) % 4
            pairs.append((row * 2 + core, to * 2 + core))
    return lax.ppermute(value, ("row", "col"), pairs)


def across(value):
    return lax.ppermute(value, "col", [(0, 1), (1, 0)])


def plane(value, phase, hop):
    pairs = []
    for core in range(2):
        for z in range(4):
            for y in range(4):
                if core == phase:
                    to = ((z + hop) % 4) * 4 + y
                else:
                    to = z * 4 + (y + hop) % 4
                pairs.append((core * 16 + z * 4 + y, core * 16 + to))
    return lax.ppermute(value, ("col", "depth"), pairs)


def held(*values):
    return lax.optimization_barrier(values)


def on_device(tokens, up_weight, down_weight, out_grad):
    x = lax.axis_index("row")
    sign = 1 - 2 * lax.axis_index("col")
    rows, width = tokens.shape
    sub = rows // 4
    hid = up_weight.shape[1]

    def pick(value, at, axis):
        return lax.dynamic_index_in_dim(value, (at + 8) % 4, axis, keepdims=False)

    both = jnp.stack([tokens, out_grad]).reshape(2, 4, sub, width).transpose(1, 0, 2, 3)
    own = lax.all_to_all(both, "row", 0, 0, tiled=True)
    own = jnp.stack(
        [
            jnp.concatenate([pick(own[:, 0], x - sign * k, 0) for k in range(4)], axis=1),
            jnp.concatenate([pick(own[:, 1], x + sign * k, 0) for k in range(4)], axis=1),
        ]
    )

    ups, downs = [up_weight], [down_weight]
    ups.append(along_x(ups[-1], 1))
    own, ups[-1] = held(own, ups[-1])

    ups.append(along_x(ups[-1], 1))
    downs.append(along_x(downs[-1], -1))
    first = jnp.concatenate([own] + [plane(own, 0, hop) for hop in (1, 2, 3)], axis=1)
    first, ups[-1], downs[-1] = held(first, ups[-1], downs[-1])

    ups.append(along_x(ups[-1], 1))
    downs.append(along_x(downs[-1], -1))
    tok, cot = [first[0]], [first[1]]
    tok.append(plane(tok[-1], 1, 1))
    cot.append(plane(cot[-1], 1, -1))
    tok[-1], cot[-1], ups[-1], downs[-1] = held(tok[-1], cot[-1], ups[-1], downs[-1])

    downs.append(along_x(downs[-1], -1))
    (up_mine,) = held(jnp.concatenate(ups, axis=0))
    up_theirs = across(up_mine)
    tok.append(plane(tok[-1], 1, 1))
    cot.append(plane(cot[-1], 1, -1))
    tok[-1], cot[-1], downs[-1], up_theirs = held(tok[-1], cot[-1], downs[-1], up_theirs)

    def theirs_in_order(value, axis):
        parts = [lax.slice_in_dim(value, k * width, (k + 1) * width, axis=axis) for k in range(4)]
        return held(jnp.concatenate([parts[0], parts[3], parts[2], parts[1]], axis=axis))[0]

    up = jnp.concatenate([up_mine, theirs_in_order(up_theirs, 0)], axis=1)
    (down_mine,) = held(jnp.concatenate(downs, axis=1))
    down = jnp.concatenate([down_mine, theirs_in_order(across(down_mine), 1)], axis=0)
    up, down = held(up, down)
    tok.append(plane(tok[-1], 1, 1))
    cot.append(plane(cot[-1], 1, -1))
    cot = [cot[0], cot[3], cot[2], cot[1]]

    hidden = [product(part, up, 1, 0) for part in tok]
    activated = [gelu_value(part).astype(BF) for part in hidden]
    act_grad = [product(part, down, 1, 1) for part in cot]
    hidden_grad = [(a * gelu_slope(h)).astype(BF) for a, h in zip(act_grad, hidden)]

    acts, hgs = jnp.concatenate(activated, axis=0), jnp.concatenate(hidden_grad, axis=0)
    feats, cots = jnp.concatenate(tok, axis=0), jnp.concatenate(cot, axis=0)

    def block(value, k):
        return lax.slice_in_dim(value, k * width, (k + 1) * width, axis=1)

    def mixed_part(j):
        return product(activated[j], down, 1, 0)

    def back_part(j):
        return product(hidden_grad[j], up, 1, 1)

    def down_part(k):
        part = product(acts[:, :hid], block(cots, k), 0, 0)
        return part + block(down_theirs, (4 - k) % 4).astype(F32)

    def up_part(k):
        at = ((4 - k) % 4) * width
        part = product(block(feats, k), hgs[:, :hid], 0, 0)
        return part + lax.slice_in_dim(up_theirs, at, at + width, axis=0).astype(F32)

    def both_steps(mixed, back, j_mixed, j_back, *others):
        mixed, back = plane(mixed, 1, 1), plane(back, 1, -1)
        mixed, back, *others = held(mixed, back, *others)
        mixed = (mixed.astype(F32) + mixed_part(j_mixed)).astype(BF)
        back = (back.astype(F32) + back_part(j_back)).astype(BF)
        return mixed, back, *others

    mixed, back = mixed_part(1).astype(BF), back_part(3).astype(BF)
    down_theirs = across(product(acts[:, hid:], cots, 0, 0).astype(BF))
    up_theirs = across(product(feats, hgs[:, hid:], 0, 0).astype(BF))
    mixed, back, down_theirs, up_theirs = both_steps(mixed, back, 2, 2, down_theirs, up_theirs)

    down_grad = along_x(down_part(1).astype(BF), -1)
    up_grad = along_x(up_part(1).astype(BF), 1)
    mixed, back, down_grad, up_grad = both_steps(mixed, back, 3, 1, down_grad, up_grad)

    down_grad = along_x((down_grad.astype(F32) + down_part(2)).astype(BF), -1)
    up_grad = along_x((up_grad.astype(F32) + up_part(2)).astype(BF), 1)
    mixed, back, down_grad, up_grad = both_steps(mixed, back, 0, 0, down_grad, up_grad)

    down_grad = along_x((down_grad.astype(F32) + down_part(3)).astype(BF), -1)
    up_grad = along_x((up_grad.astype(F32) + up_part(3)).astype(BF), 1)
    total = jnp.stack([mixed, back]).reshape(2, 4, sub, 4 * width)
    end = total[:, 0].astype(F32)
    for hop in (1, 2, 3):
        end = end + plane(total[:, hop], 0, -hop).astype(F32)
    end = end.astype(BF).reshape(2, sub, 4, width)
    end = jnp.stack(
        [
            jnp.stack([pick(end[0], sign * (at - x), 1), pick(end[1], sign * (x - at), 1)])
            for at in range(4)
        ]
    )
    out = lax.all_to_all(end, "row", 0, 0, tiled=True)
    out = out.transpose(1, 0, 2, 3).reshape(2, rows, width)
    down_grad = down_grad.astype(F32) + down_part(0)
    up_grad = up_grad.astype(F32) + up_part(0)
    return out[0], out[1], up_grad, down_grad


def solution(mesh):
    spec = P(("col", "depth"), "row")
    wide = P("row", ("col", "depth"))
    return jax.shard_map(
        on_device,
        mesh=mesh,
        in_specs=(spec, wide, spec, spec),
        out_specs=(spec, spec, wide, spec),
        check_vma=False,
    )
```

```python
import jax
import jax.numpy as jnp
from jax import lax
from jax.sharding import PartitionSpec as P

BF = jnp.bfloat16
F32 = jnp.float32


def gelu_value(value):
    return value * 0.5 * (1.0 + lax.erf(value * 0.7071067811865476))


def gelu_slope(value):
    return (
        0.5 * (1.0 + lax.erf(value * 0.7071067811865476))
        + value * jnp.exp(-0.5 * value * value) * 0.3989422804014327
    )


def product(left, right, left_dim, right_dim):
    return lax.dot_general(
        left, right, (((left_dim,), (right_dim,)), ((), ())), preferred_element_type=F32
    )


def along_x(value, hop):
    pairs = []
    for row in range(4):
        for core in range(2):
            to = (row + (hop if core == 0 else -hop)) % 4
            pairs.append((row * 2 + core, to * 2 + core))
    return lax.ppermute(value, ("row", "col"), pairs)


def across(value):
    return lax.ppermute(value, "col", [(0, 1), (1, 0)])


def plane(value, phase, hop):
    pairs = []
    for core in range(2):
        for z in range(4):
            for y in range(4):
                if core == phase:
                    to = ((z + hop) % 4) * 4 + y
                else:
                    to = z * 4 + (y + hop) % 4
                pairs.append((core * 16 + z * 4 + y, core * 16 + to))
    return lax.ppermute(value, ("col", "depth"), pairs)


def held(*values):
    return lax.optimization_barrier(values)


def on_device(tokens, up_weight, down_weight, out_grad):
    x = lax.axis_index("row")
    sign = 1 - 2 * lax.axis_index("col")
    rows, width = tokens.shape
    sub, half = rows // 4, rows // 2
    hid = up_weight.shape[1]

    def pick(value, at, axis):
        return lax.dynamic_index_in_dim(value, (at + 8) % 4, axis, keepdims=False)

    both = jnp.stack([tokens, out_grad]).reshape(2, 4, sub, width).transpose(1, 0, 2, 3)
    own = lax.all_to_all(both, "row", 0, 0, tiled=True)
    own = jnp.stack(
        [
            jnp.concatenate([pick(own[:, 0], x - sign * k, 0) for k in range(4)], axis=1),
            jnp.concatenate([pick(own[:, 1], x + sign * k, 0) for k in range(4)], axis=1),
        ]
    )

    ups, downs = [up_weight], [down_weight]
    ups.append(along_x(ups[-1], 1))
    own, ups[-1] = held(own, ups[-1])

    ups.append(along_x(ups[-1], 1))
    downs.append(along_x(downs[-1], -1))
    first = jnp.concatenate([own] + [plane(own, 0, hop) for hop in (1, 2, 3)], axis=1)
    first, ups[-1], downs[-1] = held(first, ups[-1], downs[-1])

    ups.append(along_x(ups[-1], 1))
    downs.append(along_x(downs[-1], -1))
    left, right = plane(first, 1, 1), plane(first, 1, -1)
    left, right, ups[-1], downs[-1] = held(left, right, ups[-1], downs[-1])

    downs.append(along_x(downs[-1], -1))
    (up_mine,) = held(jnp.concatenate(ups, axis=0))
    up_theirs = across(up_mine)
    far = [plane(left[:, :half], 1, 1), plane(right[:, half:], 1, -1)]
    *far, downs[-1], up_theirs = held(*far, downs[-1], up_theirs)
    far = jnp.concatenate(far, axis=1)
    tok = [part[0] for part in (first, left, far, right)]
    cot = [part[1] for part in (first, left, far, right)]

    def theirs_in_order(value, axis):
        parts = [lax.slice_in_dim(value, k * width, (k + 1) * width, axis=axis) for k in range(4)]
        return held(jnp.concatenate([parts[0], parts[3], parts[2], parts[1]], axis=axis))[0]

    up = jnp.concatenate([up_mine, theirs_in_order(up_theirs, 0)], axis=1)
    (down_mine,) = held(jnp.concatenate(downs, axis=1))
    down = jnp.concatenate([down_mine, theirs_in_order(across(down_mine), 1)], axis=0)
    up, down = held(up, down)

    hidden = [product(part, up, 1, 0) for part in tok]
    activated = [gelu_value(part).astype(BF) for part in hidden]
    act_grad = [product(part, down, 1, 1) for part in cot]
    hidden_grad = [(a * gelu_slope(h)).astype(BF) for a, h in zip(act_grad, hidden)]

    def part(j):
        mixed = product(activated[j], down, 1, 0).astype(BF)
        return jnp.stack([mixed, product(hidden_grad[j], up, 1, 1).astype(BF)])

    far = part(2)
    far, *rest = held(far, *tok, *cot, *activated, *hidden_grad)
    tok, cot, activated, hidden_grad = rest[:4], rest[4:8], rest[8:12], rest[12:]
    acts, hgs = jnp.concatenate(activated, axis=0), jnp.concatenate(hidden_grad, axis=0)
    feats, cots = jnp.concatenate(tok, axis=0), jnp.concatenate(cot, axis=0)

    def columns(value, k):
        return lax.slice_in_dim(value, k * width, (k + 1) * width, axis=1)

    far = [plane(far[:, :half], 1, -1), plane(far[:, half:], 1, 1)]
    left, right = part(1), part(3)
    *far, left, right = held(*far, left, right)
    down_theirs = across(product(acts[:, hid:], cots, 0, 0).astype(BF))
    up_theirs = across(product(feats, hgs[:, hid:], 0, 0).astype(BF))

    def plus(one, other):
        return (one.astype(F32) + other.astype(F32)).astype(BF)

    left = jnp.concatenate([plus(left[:, :half], far[0]), left[:, half:]], axis=1)
    right = jnp.concatenate([right[:, :half], plus(right[:, half:], far[1])], axis=1)
    left, right = plane(left, 1, -1), plane(right, 1, 1)

    def down_part(k):
        mine = product(acts[:, :hid], columns(cots, k), 0, 0)
        return mine + columns(down_theirs, (4 - k) % 4).astype(F32)

    def up_part(k):
        at = ((4 - k) % 4) * width
        mine = product(columns(feats, k), hgs[:, :hid], 0, 0)
        return mine + lax.slice_in_dim(up_theirs, at, at + width, axis=0).astype(F32)

    down_grad = along_x(down_part(1).astype(BF), -1)
    up_grad = along_x(up_part(1).astype(BF), 1)
    here, down_next, up_next = part(0), down_part(2), up_part(2)
    left, right, here, down_grad, up_grad, down_next, up_next = held(
        left, right, here, down_grad, up_grad, down_next, up_next
    )

    total = (here.astype(F32) + left.astype(F32) + right.astype(F32)).astype(BF)
    total = total.reshape(2, 4, sub, 4 * width)
    end = total[:, 0].astype(F32)
    for hop in (1, 2, 3):
        end = end + plane(total[:, hop], 0, -hop).astype(F32)
    down_grad = along_x((down_grad.astype(F32) + down_next).astype(BF), -1)
    up_grad = along_x((up_grad.astype(F32) + up_next).astype(BF), 1)
    down_next, up_next = down_part(3), up_part(3)
    end, down_grad, up_grad, down_next, up_next = held(
        end, down_grad, up_grad, down_next, up_next
    )

    down_grad = along_x((down_grad.astype(F32) + down_next).astype(BF), -1)
    up_grad = along_x((up_grad.astype(F32) + up_next).astype(BF), 1)
    down_next, up_next = down_part(0), up_part(0)
    down_grad, up_grad, down_next, up_next = held(down_grad, up_grad, down_next, up_next)
    end = end.astype(BF).reshape(2, sub, 4, width)
    end = jnp.stack(
        [
            jnp.stack([pick(end[0], sign * (at - x), 1), pick(end[1], sign * (x - at), 1)])
            for at in range(4)
        ]
    )
    out = lax.all_to_all(end, "row", 0, 0, tiled=True)
    out = out.transpose(1, 0, 2, 3).reshape(2, rows, width)
    down_grad = down_grad.astype(F32) + down_next
    up_grad = up_grad.astype(F32) + up_next
    return out[0], out[1], up_grad, down_grad


def solution(mesh):
    spec = P(("col", "depth"), "row")
    wide = P("row", ("col", "depth"))
    return jax.shard_map(
        on_device,
        mesh=mesh,
        in_specs=(spec, wide, spec, spec),
        out_specs=(spec, spec, wide, spec),
        check_vma=False,
    )
```

```python
import jax
import jax.numpy as jnp
from jax import lax
from jax.experimental import pallas as pl
from jax.experimental.pallas import tpu as pltpu
from jax.sharding import PartitionSpec as P

BF = jnp.bfloat16
F32 = jnp.float32


def gelu_value(value):
    return value * 0.5 * (1.0 + lax.erf(value * 0.7071067811865476))


def gelu_slope(value):
    return (
        0.5 * (1.0 + lax.erf(value * 0.7071067811865476))
        + value * jnp.exp(-0.5 * value * value) * 0.3989422804014327
    )


def product(left, right, left_dim, right_dim):
    return lax.dot_general(
        left, right, (((left_dim,), (right_dim,)), ((), ())), preferred_element_type=F32
    )


def local_kernel(body, grid, in_specs, out_specs, out_shape, *arrays):
    return pl.pallas_call(
        body,
        grid=grid,
        in_specs=in_specs,
        out_specs=out_specs,
        out_shape=out_shape,
        compiler_params=pltpu.CompilerParams(vmem_limit_bytes=40 * 2**20),
        cost_estimate=pl.CostEstimate(flops=1, bytes_accessed=1, transcendentals=0),
    )(*arrays)


def forward(pair, up, down):
    _, rows, features = pair.shape
    units = up.shape[1]
    tile = units // 3

    def body(pair_ref, up_ref, down_ref, act_ref, grad_ref):
        hidden = product(pair_ref[0], up_ref[...], 1, 0)
        act_grad = product(pair_ref[1], down_ref[...], 1, 1)
        act_ref[...] = gelu_value(hidden).astype(BF)
        grad_ref[...] = (act_grad * gelu_slope(hidden)).astype(BF)

    out = pl.BlockSpec((rows, tile), lambda i: (0, i))
    shape = jax.ShapeDtypeStruct((rows, units), BF)
    return local_kernel(
        body,
        (3,),
        [
            pl.BlockSpec((2, rows, features), lambda i: (0, 0, 0)),
            pl.BlockSpec((features, tile), lambda i: (0, i)),
            pl.BlockSpec((tile, features), lambda i: (i, 0)),
        ],
        [out, out],
        [shape, shape],
        pair,
        up,
        down,
    )


def backward(acts, grads, up, down):
    rows, units = acts.shape
    features = up.shape[0]
    tile = features // 4

    def body(act_ref, grad_ref, up_ref, down_ref, out_ref):
        out_ref[0] = product(act_ref[...], down_ref[...], 1, 0).astype(BF)
        out_ref[1] = product(grad_ref[...], up_ref[...], 1, 1).astype(BF)

    whole = pl.BlockSpec((rows, units), lambda i: (0, 0))
    return local_kernel(
        body,
        (4,),
        [
            whole,
            whole,
            pl.BlockSpec((tile, units), lambda i: (i, 0)),
            pl.BlockSpec((units, tile), lambda i: (0, i)),
        ],
        pl.BlockSpec((2, rows, tile), lambda i: (0, 0, i)),
        jax.ShapeDtypeStruct((2, rows, features), BF),
        acts,
        grads,
        up,
        down,
    )


def weight_sums(sets, acts, grads, core):
    units = acts[0].shape[1] // 2
    features = sets[0].shape[2]
    tile = features // 4
    count = len(sets)

    def body(*refs):
        down_ref, up_ref = refs[-2:]
        down_sum = up_sum = None
        for i in range(count):
            down_part = product(refs[count + i][...], refs[i][1], 0, 0)
            up_part = product(refs[i][0], refs[2 * count + i][...], 0, 0)
            down_sum = down_part if i == 0 else down_sum + down_part
            up_sum = up_part if i == 0 else up_sum + up_part
        down_ref[...] = down_sum.astype(BF)
        up_ref[...] = up_sum.astype(BF)

    halves = [pl.BlockSpec((a.shape[0], units), lambda i: (0, core)) for a in acts]
    return local_kernel(
        body,
        (4,),
        [pl.BlockSpec((2, s.shape[1], tile), lambda i: (0, 0, i)) for s in sets] + halves + halves,
        [
            pl.BlockSpec((units, tile), lambda i: (0, i)),
            pl.BlockSpec((tile, units), lambda i: (i, 0)),
        ],
        [
            jax.ShapeDtypeStruct((units, features), BF),
            jax.ShapeDtypeStruct((features, units), BF),
        ],
        *sets,
        *acts,
        *grads,
    )


def along_x(value, hop):
    pairs = []
    for row in range(4):
        for core in range(2):
            to = (row + (hop if core == 0 else -hop)) % 4
            pairs.append((row * 2 + core, to * 2 + core))
    return lax.ppermute(value, ("row", "col"), pairs)


def across(value):
    return lax.ppermute(value, "col", [(0, 1), (1, 0)])


def plane(value, phase, hop):
    pairs = []
    for core in range(2):
        for z in range(4):
            for y in range(4):
                if core == phase:
                    to = ((z + hop) % 4) * 4 + y
                else:
                    to = z * 4 + (y + hop) % 4
                pairs.append((core * 16 + z * 4 + y, core * 16 + to))
    return lax.ppermute(value, ("col", "depth"), pairs)


def held(*values):
    return lax.optimization_barrier(values)


def on_device(tokens, up_weight, down_weight, out_grad):
    x = lax.axis_index("row")
    sign = 1 - 2 * lax.axis_index("col")
    rows, width = tokens.shape
    sub, half = rows // 4, rows // 2
    hid = up_weight.shape[1]

    turned = (0, 3, 2, 1)

    both = jnp.stack([tokens, out_grad]).reshape(2, 4, sub, width)

    def piece(k):
        return lax.dynamic_index_in_dim(both, (x + sign * k + 4) % 4, 1, keepdims=False)

    got = [piece(0)] + [along_x(piece(k), k) for k in (1, 2, 3)]
    own = jnp.stack(
        [
            jnp.concatenate([got[k][0] for k in range(4)], axis=1),
            jnp.concatenate([got[k][1] for k in turned], axis=1),
        ]
    )

    ups, downs = [up_weight], [down_weight]
    ups.append(along_x(ups[-1], 1))
    own, ups[1] = held(own, ups[1])

    ups.append(along_x(ups[1], 1))
    downs.append(along_x(downs[0], -1))
    first = jnp.concatenate([own] + [plane(own, 0, hop) for hop in (1, 2, 3)], axis=1)
    first, ups[2], downs[1] = held(first, ups[2], downs[1])

    def join(parts, axis):
        return parts[0] if len(parts) == 1 else jnp.concatenate(parts, axis=axis)

    ups.append(along_x(ups[2], 1))
    downs.append(along_x(downs[1], -1))
    downs.append(along_x(downs[2], -1))
    up_early, down_early = across(join(ups[:3], 0)), across(join(downs[:2], 1))
    left, right = plane(first, 1, 1), plane(first, 1, -1)
    left, right, ups[3], downs[2], downs[3], up_early, down_early = held(
        left, right, ups[3], downs[2], downs[3], up_early, down_early
    )

    far = [plane(left[:, :half], 1, 1), plane(right[:, half:], 1, -1)]
    up_late, down_late = across(ups[3]), across(join(downs[2:], 1))

    def rows_of(value, k):
        return lax.slice_in_dim(value, k * width, (k + 1) * width, axis=0)

    def columns(value, k):
        return lax.slice_in_dim(value, k * width, (k + 1) * width, axis=1)

    up = held(
        join(ups, 0), join([rows_of(up_early, 0), up_late, up_early[2 * width :], rows_of(up_early, 1)], 0)
    )
    down = held(
        join(downs, 1),
        join([columns(down_early, 0), columns(down_late, 1), columns(down_late, 0), columns(down_early, 1)], 1),
    )
    up, down = held(join(up, 1), join(down, 0))

    near = join([first, left, right], 1)
    near_acts, near_grads = forward(near, up, down)
    *far, near_acts, near_grads = held(*far, near_acts, near_grads)
    far = join(far, 1)
    far_acts, far_grads = forward(far, up, down)

    far_sums = backward(far_acts, far_grads, up, down)
    far_sums, near_acts, near_grads, far_acts, far_grads = held(
        far_sums, near_acts, near_grads, far_acts, far_grads
    )
    far_back = [plane(far_sums[:, :half], 1, -1), plane(far_sums[:, half:], 1, 1)]
    sets, acts, grads = (near, far), (near_acts, far_acts), (near_grads, far_grads)
    down_theirs, up_theirs = (across(value) for value in weight_sums(sets, acts, grads, 1))
    near_sums = backward(near_acts, near_grads, up, down)
    down_mine, up_mine = weight_sums(sets, acts, grads, 0)
    *far_back, near_sums, down_theirs, up_theirs, down_mine, up_mine = held(
        *far_back, near_sums, down_theirs, up_theirs, down_mine, up_mine
    )

    def total(*parts):
        value = parts[0].astype(F32)
        for part in parts[1:]:
            value = value + part.astype(F32)
        return value

    here, left, right = (near_sums[:, i * rows : (i + 1) * rows] for i in range(3))
    left = join([total(left[:, :half], far_back[0]).astype(BF), left[:, half:]], 1)
    right = join([right[:, :half], total(right[:, half:], far_back[1]).astype(BF)], 1)
    left, right = plane(left, 1, -1), plane(right, 1, 1)

    def down_part(k, *more):
        return total(columns(down_mine, k), columns(down_theirs, turned[k]), *more)

    def up_part(k, *more):
        return total(rows_of(up_mine, k), rows_of(up_theirs, turned[k]), *more)

    down_grad = along_x(down_part(1).astype(BF), -1)
    up_grad = along_x(up_part(1).astype(BF), 1)
    down_grad = along_x(down_part(2, down_grad).astype(BF), -1)
    up_grad = along_x(up_part(2, up_grad).astype(BF), 1)
    left, right, down_grad, up_grad = held(left, right, down_grad, up_grad)

    sums = total(here, left, right).astype(BF).reshape(2, 4, sub, 4 * width)
    down_grad = along_x(down_part(3, down_grad).astype(BF), -1)
    up_grad = along_x(up_part(3, up_grad).astype(BF), 1)
    end = total(sums[:, 0], *(plane(sums[:, hop], 0, -hop) for hop in (1, 2, 3)))
    end, down_grad, up_grad = held(end.astype(BF), down_grad, up_grad)
    down_grad, up_grad = down_part(0, down_grad), up_part(0, up_grad)

    out = jnp.zeros((2, rows, width), BF)
    for k in range(4):
        sent = jnp.stack([columns(end[0], turned[k]), columns(end[1], k)])
        got = along_x(sent, -k) if k else sent
        at = (x + sign * k + 4) % 4 * sub
        out = lax.dynamic_update_slice_in_dim(out, got, at, axis=1)
    return out[0], out[1], up_grad, down_grad


def solution(mesh):
    spec = P(("col", "depth"), "row")
    wide = P("row", ("col", "depth"))
    return jax.shard_map(
        on_device,
        mesh=mesh,
        in_specs=(spec, wide, spec, spec),
        out_specs=(spec, spec, wide, spec),
        check_vma=False,
    )
```

```python
import jax
import jax.numpy as jnp
from jax import lax
from jax.experimental import pallas as pl
from jax.experimental.pallas import tpu as pltpu
from jax.sharding import PartitionSpec as P

BF = jnp.bfloat16
F32 = jnp.float32


def gelu_value(value):
    return value * 0.5 * (1.0 + lax.erf(value * 0.7071067811865476))


def gelu_slope(value):
    return (
        0.5 * (1.0 + lax.erf(value * 0.7071067811865476))
        + value * jnp.exp(-0.5 * value * value) * 0.3989422804014327
    )


def product(left, right, left_dim, right_dim):
    return lax.dot_general(
        left, right, (((left_dim,), (right_dim,)), ((), ())), preferred_element_type=F32
    )


def local_kernel(body, grid, in_specs, out_specs, out_shape, *arrays):
    return pl.pallas_call(
        body,
        grid=grid,
        in_specs=in_specs,
        out_specs=out_specs,
        out_shape=out_shape,
        compiler_params=pltpu.CompilerParams(vmem_limit_bytes=40 * 2**20),
        cost_estimate=pl.CostEstimate(flops=1, bytes_accessed=1, transcendentals=0),
    )(*arrays)


def forward(pair, up, down):
    _, rows, features = pair.shape
    units = up.shape[1]
    tile = units // 3

    def body(pair_ref, up_ref, down_ref, act_ref, grad_ref):
        hidden = product(pair_ref[0], up_ref[...], 1, 0)
        act_grad = product(pair_ref[1], down_ref[...], 1, 1)
        act_ref[...] = gelu_value(hidden).astype(BF)
        grad_ref[...] = (act_grad * gelu_slope(hidden)).astype(BF)

    out = pl.BlockSpec((rows, tile), lambda i: (0, i))
    shape = jax.ShapeDtypeStruct((rows, units), BF)
    return local_kernel(
        body,
        (3,),
        [
            pl.BlockSpec((2, rows, features), lambda i: (0, 0, 0)),
            pl.BlockSpec((features, tile), lambda i: (0, i)),
            pl.BlockSpec((tile, features), lambda i: (i, 0)),
        ],
        [out, out],
        [shape, shape],
        pair,
        up,
        down,
    )


def backward(acts, grads, up, down):
    rows, units = acts.shape
    features = up.shape[0]
    tile = features // 4

    def body(act_ref, grad_ref, up_ref, down_ref, out_ref):
        out_ref[0] = product(act_ref[...], down_ref[...], 1, 0).astype(BF)
        out_ref[1] = product(grad_ref[...], up_ref[...], 1, 1).astype(BF)

    whole = pl.BlockSpec((rows, units), lambda i: (0, 0))
    return local_kernel(
        body,
        (4,),
        [
            whole,
            whole,
            pl.BlockSpec((tile, units), lambda i: (i, 0)),
            pl.BlockSpec((units, tile), lambda i: (0, i)),
        ],
        pl.BlockSpec((2, rows, tile), lambda i: (0, 0, i)),
        jax.ShapeDtypeStruct((2, rows, features), BF),
        acts,
        grads,
        up,
        down,
    )


def weight_sums(sets, acts, grads, core):
    units = acts[0].shape[1] // 2
    features = sets[0].shape[2]
    tile = features // 4
    count = len(sets)

    def body(*refs):
        down_ref, up_ref = refs[-2:]
        down_sum = up_sum = None
        for i in range(count):
            down_part = product(refs[count + i][...], refs[i][1], 0, 0)
            up_part = product(refs[i][0], refs[2 * count + i][...], 0, 0)
            down_sum = down_part if i == 0 else down_sum + down_part
            up_sum = up_part if i == 0 else up_sum + up_part
        down_ref[...] = down_sum.astype(BF)
        up_ref[...] = up_sum.astype(BF)

    halves = [pl.BlockSpec((a.shape[0], units), lambda i: (0, core)) for a in acts]
    return local_kernel(
        body,
        (4,),
        [pl.BlockSpec((2, s.shape[1], tile), lambda i: (0, 0, i)) for s in sets] + halves + halves,
        [
            pl.BlockSpec((units, tile), lambda i: (0, i)),
            pl.BlockSpec((tile, units), lambda i: (i, 0)),
        ],
        [
            jax.ShapeDtypeStruct((units, features), BF),
            jax.ShapeDtypeStruct((features, units), BF),
        ],
        *sets,
        *acts,
        *grads,
    )


def along_x(value, hop):
    pairs = []
    for row in range(4):
        for core in range(2):
            to = (row + (hop if core == 0 else -hop)) % 4
            pairs.append((row * 2 + core, to * 2 + core))
    return lax.ppermute(value, ("row", "col"), pairs)


def across(value):
    return lax.ppermute(value, "col", [(0, 1), (1, 0)])


def plane(value, phase, hop):
    pairs = []
    for core in range(2):
        for z in range(4):
            for y in range(4):
                if core == phase:
                    to = ((z + hop) % 4) * 4 + y
                else:
                    to = z * 4 + (y + hop) % 4
                pairs.append((core * 16 + z * 4 + y, core * 16 + to))
    return lax.ppermute(value, ("col", "depth"), pairs)


def held(*values):
    return lax.optimization_barrier(values)


def on_device(tokens, up_weight, down_weight, out_grad):
    x = lax.axis_index("row")
    sign = 1 - 2 * lax.axis_index("col")
    rows, width = tokens.shape
    sub, half = rows // 4, rows // 2
    hid = up_weight.shape[1]

    turned = (0, 3, 2, 1)

    both = jnp.stack([tokens, out_grad]).reshape(2, 4, sub, width)

    def piece(k):
        return lax.dynamic_index_in_dim(both, (x + sign * k + 4) % 4, 1, keepdims=False)

    got = [piece(0)] + [along_x(piece(k), k) for k in (1, 2, 3)]
    own = jnp.stack(
        [
            jnp.concatenate([got[k][0] for k in range(4)], axis=1),
            jnp.concatenate([got[k][1] for k in turned], axis=1),
        ]
    )

    ups, downs = [up_weight], [down_weight]

    def step(*values):
        ups.append(along_x(ups[-1], 1))
        downs.append(along_x(downs[-1], -1))
        *values, ups[-1], downs[-1] = held(*values, ups[-1], downs[-1])
        return values

    def join(parts, axis):
        return jnp.concatenate(parts, axis=axis)

    (own,) = step(own)
    (first,) = step(join([own] + [plane(own, 0, hop) for hop in (1, 2, 3)], 1))

    up_early = across(join(ups[:3], 0))
    left, right = plane(first, 1, 1), plane(first, 1, -1)
    left, right, up_early = step(left, right, up_early)
    (down_mine,) = held(join(downs, 1))
    up_late, down_theirs = across(ups[3]), across(down_mine)
    far = [plane(left[:, :half], 1, 1), plane(right[:, half:], 1, -1)]

    def rows_of(value, k):
        return lax.slice_in_dim(value, k * width, (k + 1) * width, axis=0)

    def columns(value, k):
        return lax.slice_in_dim(value, k * width, (k + 1) * width, axis=1)

    up = held(
        join(ups, 0),
        join([rows_of(up_early, 0), up_late, rows_of(up_early, 2), rows_of(up_early, 1)], 0),
    )
    down = held(down_mine, join([columns(down_theirs, k) for k in turned], 1))
    up, down = held(join(up, 1), join(down, 0))

    near = join([first, left, right], 1)
    near_acts, near_grads = forward(near, up, down)
    *far, near_acts, near_grads = held(*far, near_acts, near_grads)
    far = join(far, 1)
    far_acts, far_grads = forward(far, up, down)

    far_sums = backward(far_acts, far_grads, up, down)
    far_sums, near_acts, near_grads, far_acts, far_grads = held(
        far_sums, near_acts, near_grads, far_acts, far_grads
    )
    far_back = [plane(far_sums[:, :half], 1, -1), plane(far_sums[:, half:], 1, 1)]
    sets, acts, grads = (near, far), (near_acts, far_acts), (near_grads, far_grads)
    down_theirs, up_theirs = (across(value) for value in weight_sums(sets, acts, grads, 1))
    near_sums = backward(near_acts, near_grads, up, down)
    down_mine, up_mine = weight_sums(sets, acts, grads, 0)
    *far_back, near_sums, down_mine, up_mine = held(*far_back, near_sums, down_mine, up_mine)

    def total(*parts):
        value = parts[0].astype(F32)
        for part in parts[1:]:
            value = value + part.astype(F32)
        return value

    here, left, right = (near_sums[:, i * rows : (i + 1) * rows] for i in range(3))
    left = join([total(left[:, :half], far_back[0]).astype(BF), left[:, half:]], 1)
    right = join([right[:, :half], total(right[:, half:], far_back[1]).astype(BF)], 1)
    left, right = plane(left, 1, -1), plane(right, 1, 1)

    def down_part(k, *more):
        return total(columns(down_mine, k), columns(down_theirs, turned[k]), *more)

    def up_part(k, *more):
        return total(rows_of(up_mine, k), rows_of(up_theirs, turned[k]), *more)

    down_grad = along_x(down_part(1).astype(BF), -1)
    up_grad = along_x(up_part(1).astype(BF), 1)
    left, right, down_grad, up_grad = held(left, right, down_grad, up_grad)

    down_grad = along_x(down_part(2, down_grad).astype(BF), -1)
    up_grad = along_x(up_part(2, up_grad).astype(BF), 1)
    sums = total(here, left, right).astype(BF).reshape(2, 4, sub, 4 * width)
    end = total(sums[:, 0], *(plane(sums[:, hop], 0, -hop) for hop in (1, 2, 3)))
    end, down_grad, up_grad = held(end.astype(BF), down_grad, up_grad)
    down_grad = along_x(down_part(3, down_grad).astype(BF), -1)
    up_grad = along_x(up_part(3, up_grad).astype(BF), 1)
    down_grad, up_grad = down_part(0, down_grad), up_part(0, up_grad)

    out = jnp.zeros((2, rows, width), BF)
    for k in range(4):
        sent = jnp.stack([columns(end[0], turned[k]), columns(end[1], k)])
        got = along_x(sent, -k) if k else sent
        at = (x + sign * k + 4) % 4 * sub
        out = lax.dynamic_update_slice_in_dim(out, got, at, axis=1)
    return out[0], out[1], up_grad, down_grad


def solution(mesh):
    spec = P(("col", "depth"), "row")
    wide = P("row", ("col", "depth"))
    return jax.shard_map(
        on_device,
        mesh=mesh,
        in_specs=(spec, wide, spec, spec),
        out_specs=(spec, spec, wide, spec),
        check_vma=False,
    )
```

```python
import jax
import jax.numpy as jnp
from jax import lax
from jax.experimental import pallas as pl
from jax.experimental.pallas import tpu as pltpu
from jax.sharding import PartitionSpec as P

BF = jnp.bfloat16
F32 = jnp.float32


def gelu_value(value):
    return value * 0.5 * (1.0 + lax.erf(value * 0.7071067811865476))


def gelu_slope(value):
    return (
        0.5 * (1.0 + lax.erf(value * 0.7071067811865476))
        + value * jnp.exp(-0.5 * value * value) * 0.3989422804014327
    )


def product(left, right, left_dim, right_dim):
    return lax.dot_general(
        left, right, (((left_dim,), (right_dim,)), ((), ())), preferred_element_type=F32
    )


def local_kernel(body, grid, in_specs, out_specs, out_shape, *arrays):
    return pl.pallas_call(
        body,
        grid=grid,
        in_specs=in_specs,
        out_specs=out_specs,
        out_shape=out_shape,
        compiler_params=pltpu.CompilerParams(vmem_limit_bytes=40 * 2**20),
        cost_estimate=pl.CostEstimate(flops=1, bytes_accessed=1, transcendentals=0),
    )(*arrays)


def forward(pair, up, down):
    _, rows, features = pair.shape
    units = up.shape[1]
    tile = units // 3

    def body(pair_ref, up_ref, down_ref, act_ref, grad_ref):
        hidden = product(pair_ref[0], up_ref[...], 1, 0)
        act_grad = product(pair_ref[1], down_ref[...], 1, 1)
        act_ref[...] = gelu_value(hidden).astype(BF)
        grad_ref[...] = (act_grad * gelu_slope(hidden)).astype(BF)

    out = pl.BlockSpec((rows, tile), lambda i: (0, i))
    shape = jax.ShapeDtypeStruct((rows, units), BF)
    return local_kernel(
        body,
        (3,),
        [
            pl.BlockSpec((2, rows, features), lambda i: (0, 0, 0)),
            pl.BlockSpec((features, tile), lambda i: (0, i)),
            pl.BlockSpec((tile, features), lambda i: (i, 0)),
        ],
        [out, out],
        [shape, shape],
        pair,
        up,
        down,
    )


def backward(acts, grads, up, down):
    rows, units = acts.shape
    features = up.shape[0]
    tile = features // 4

    def body(act_ref, grad_ref, up_ref, down_ref, out_ref):
        out_ref[0] = product(act_ref[...], down_ref[...], 1, 0).astype(BF)
        out_ref[1] = product(grad_ref[...], up_ref[...], 1, 1).astype(BF)

    whole = pl.BlockSpec((rows, units), lambda i: (0, 0))
    return local_kernel(
        body,
        (4,),
        [
            whole,
            whole,
            pl.BlockSpec((tile, units), lambda i: (i, 0)),
            pl.BlockSpec((units, tile), lambda i: (0, i)),
        ],
        pl.BlockSpec((2, rows, tile), lambda i: (0, 0, i)),
        jax.ShapeDtypeStruct((2, rows, features), BF),
        acts,
        grads,
        up,
        down,
    )


def weight_sums(sets, acts, grads, core):
    units = acts[0].shape[1] // 2
    features = sets[0].shape[2]
    tile = features // 4
    count = len(sets)

    def body(*refs):
        down_ref, up_ref = refs[-2:]
        down_sum = up_sum = None
        for i in range(count):
            down_part = product(refs[count + i][...], refs[i][1], 0, 0)
            up_part = product(refs[i][0], refs[2 * count + i][...], 0, 0)
            down_sum = down_part if i == 0 else down_sum + down_part
            up_sum = up_part if i == 0 else up_sum + up_part
        down_ref[...] = down_sum.astype(BF)
        up_ref[...] = up_sum.astype(BF)

    halves = [pl.BlockSpec((a.shape[0], units), lambda i: (0, core)) for a in acts]
    return local_kernel(
        body,
        (4,),
        [pl.BlockSpec((2, s.shape[1], tile), lambda i: (0, 0, i)) for s in sets] + halves + halves,
        [
            pl.BlockSpec((units, tile), lambda i: (0, i)),
            pl.BlockSpec((tile, units), lambda i: (i, 0)),
        ],
        [
            jax.ShapeDtypeStruct((units, features), BF),
            jax.ShapeDtypeStruct((features, units), BF),
        ],
        *sets,
        *acts,
        *grads,
    )


def along_x(value, hop):
    pairs = []
    for row in range(4):
        for core in range(2):
            to = (row + (hop if core == 0 else -hop)) % 4
            pairs.append((row * 2 + core, to * 2 + core))
    return lax.ppermute(value, ("row", "col"), pairs)


def across(value):
    return lax.ppermute(value, "col", [(0, 1), (1, 0)])


def plane(value, phase, hop):
    pairs = []
    for core in range(2):
        for z in range(4):
            for y in range(4):
                if core == phase:
                    to = ((z + hop) % 4) * 4 + y
                else:
                    to = z * 4 + (y + hop) % 4
                pairs.append((core * 16 + z * 4 + y, core * 16 + to))
    return lax.ppermute(value, ("col", "depth"), pairs)


def held(*values):
    return lax.optimization_barrier(values)


def on_device(tokens, up_weight, down_weight, out_grad):
    x = lax.axis_index("row")
    sign = 1 - 2 * lax.axis_index("col")
    rows, width = tokens.shape
    sub, half = rows // 4, rows // 2
    hid = up_weight.shape[1]

    turned = (0, 3, 2, 1)

    both = jnp.stack([tokens, out_grad]).reshape(2, 4, sub, width)

    def piece(k):
        return lax.dynamic_index_in_dim(both, (x + sign * k + 4) % 4, 1, keepdims=False)

    got = [piece(0)] + [along_x(piece(k), k) for k in (1, 2, 3)]
    own = jnp.stack(
        [
            jnp.concatenate([got[k][0] for k in range(4)], axis=1),
            jnp.concatenate([got[k][1] for k in turned], axis=1),
        ]
    )

    ups, downs = [up_weight], [down_weight]

    def step():
        ups.append(along_x(ups[-1], 1))
        downs.append(along_x(downs[-1], -1))

    def join(parts, axis):
        return jnp.concatenate(parts, axis=axis)

    step()
    own, ups[0], downs[0] = held(own, ups[0], downs[0])
    step()
    first = join([own] + [plane(own, 0, hop) for hop in (1, 2, 3)], 1)
    first, ups[1], downs[1] = held(first, ups[1], downs[1])

    up_early = across(join(ups[:3], 0))
    left, right = plane(first, 1, 1), plane(first, 1, -1)
    step()
    left, right, up_early, ups[3], downs[3] = held(left, right, up_early, ups[3], downs[3])
    (down_mine,) = held(join(downs, 1))
    up_late, down_theirs = across(ups[3]), across(down_mine)
    far = [plane(left[:, :half], 1, 1), plane(right[:, half:], 1, -1)]

    def rows_of(value, k):
        return lax.slice_in_dim(value, k * width, (k + 1) * width, axis=0)

    def columns(value, k):
        return lax.slice_in_dim(value, k * width, (k + 1) * width, axis=1)

    up = held(
        join(ups, 0),
        join([rows_of(up_early, 0), up_late, rows_of(up_early, 2), rows_of(up_early, 1)], 0),
    )
    down = held(down_mine, join([columns(down_theirs, k) for k in turned], 1))
    up, down = held(join(up, 1), join(down, 0))

    near = join([first, left, right], 1)
    near_acts, near_grads = forward(near, up, down)
    *far, near_acts, near_grads = held(*far, near_acts, near_grads)
    far = join(far, 1)
    far_acts, far_grads = forward(far, up, down)

    far_sums = backward(far_acts, far_grads, up, down)
    far_back = [far_sums[:, :half], far_sums[:, half:]]
    *far_back, near_acts, near_grads, far_acts, far_grads = held(
        *far_back, near_acts, near_grads, far_acts, far_grads
    )
    far_back = [plane(far_back[0], 1, -1), plane(far_back[1], 1, 1)]
    sets, acts, grads = (near, far), (near_acts, far_acts), (near_grads, far_grads)
    theirs = weight_sums(sets, acts, grads, 1)
    near_acts, near_grads, *theirs = held(near_acts, near_grads, *theirs)
    down_theirs, up_theirs = (across(value) for value in theirs)
    near_sums = backward(near_acts, near_grads, up, down)
    acts, grads = (near_acts, far_acts), (near_grads, far_grads)
    down_mine, up_mine = weight_sums(sets, acts, grads, 0)
    *far_back, near_sums, down_mine, up_mine, down_theirs, up_theirs = held(
        *far_back, near_sums, down_mine, up_mine, down_theirs, up_theirs
    )

    def total(*parts):
        value = parts[0].astype(F32)
        for part in parts[1:]:
            value = value + part.astype(F32)
        return value

    here, left, right = (near_sums[:, i * rows : (i + 1) * rows] for i in range(3))
    left = join([total(left[:, :half], far_back[0]).astype(BF), left[:, half:]], 1)
    right = join([right[:, :half], total(right[:, half:], far_back[1]).astype(BF)], 1)
    left, right = plane(left, 1, -1), plane(right, 1, 1)

    def down_part(k, *more):
        return total(columns(down_mine, k), columns(down_theirs, turned[k]), *more)

    def up_part(k, *more):
        return total(rows_of(up_mine, k), rows_of(up_theirs, turned[k]), *more)

    down_grad = along_x(down_part(1).astype(BF), -1)
    up_grad = along_x(up_part(1).astype(BF), 1)
    left, right, down_grad, up_grad = held(left, right, down_grad, up_grad)

    down_grad = along_x(down_part(2, down_grad).astype(BF), -1)
    up_grad = along_x(up_part(2, up_grad).astype(BF), 1)
    sums = total(here, left, right).astype(BF).reshape(2, 4, sub, 4 * width)
    end = total(sums[:, 0], *(plane(sums[:, hop], 0, -hop) for hop in (1, 2, 3)))
    end, down_grad, up_grad = held(end.astype(BF), down_grad, up_grad)
    down_grad = along_x(down_part(3, down_grad).astype(BF), -1)
    up_grad = along_x(up_part(3, up_grad).astype(BF), 1)
    down_grad, up_grad = down_part(0, down_grad), up_part(0, up_grad)

    out = jnp.zeros((2, rows, width), BF)
    for k in range(4):
        sent = jnp.stack([columns(end[0], turned[k]), columns(end[1], k)])
        got = along_x(sent, -k) if k else sent
        at = (x + sign * k + 4) % 4 * sub
        out = lax.dynamic_update_slice_in_dim(out, got, at, axis=1)
    return out[0], out[1], up_grad, down_grad


def solution(mesh):
    spec = P(("col", "depth"), "row")
    wide = P("row", ("col", "depth"))
    return jax.shard_map(
        on_device,
        mesh=mesh,
        in_specs=(spec, wide, spec, spec),
        out_specs=(spec, spec, wide, spec),
        check_vma=False,
    )
```

```python
import jax
import jax.numpy as jnp
from jax import lax
from jax.experimental import pallas as pl
from jax.experimental.pallas import tpu as pltpu
from jax.sharding import PartitionSpec as P

BF = jnp.bfloat16
F32 = jnp.float32


def gelu_value(value):
    return value * 0.5 * (1.0 + lax.erf(value * 0.7071067811865476))


def gelu_slope(value):
    return (
        0.5 * (1.0 + lax.erf(value * 0.7071067811865476))
        + value * jnp.exp(-0.5 * value * value) * 0.3989422804014327
    )


def product(left, right, left_dim, right_dim):
    return lax.dot_general(
        left, right, (((left_dim,), (right_dim,)), ((), ())), preferred_element_type=F32
    )


def local_kernel(body, grid, in_specs, out_specs, out_shape, *arrays):
    return pl.pallas_call(
        body,
        grid=grid,
        in_specs=in_specs,
        out_specs=out_specs,
        out_shape=out_shape,
        compiler_params=pltpu.CompilerParams(vmem_limit_bytes=16 * 2**20),
        cost_estimate=pl.CostEstimate(flops=1, bytes_accessed=1, transcendentals=0),
    )(*arrays)


def forward(pair, up, down):
    _, rows, features = pair.shape
    units = up.shape[1]
    tile = units // 3

    def body(pair_ref, up_ref, down_ref, act_ref, grad_ref):
        hidden = product(pair_ref[0], up_ref[...], 1, 0)
        act_grad = product(pair_ref[1], down_ref[...], 1, 1)
        act_ref[...] = gelu_value(hidden).astype(BF)
        grad_ref[...] = (act_grad * gelu_slope(hidden)).astype(BF)

    out = pl.BlockSpec((rows, tile), lambda i: (0, i))
    shape = jax.ShapeDtypeStruct((rows, units), BF)
    return local_kernel(
        body,
        (3,),
        [
            pl.BlockSpec((2, rows, features), lambda i: (0, 0, 0), pipeline_mode=pl.Buffered(1)),
            pl.BlockSpec((features, tile), lambda i: (0, i)),
            pl.BlockSpec((tile, features), lambda i: (i, 0)),
        ],
        [out, out],
        [shape, shape],
        pair,
        up,
        down,
    )


def backward(acts, grads, up, down):
    rows, units = acts.shape
    features = up.shape[0]
    tile = features // 4

    def body(act_ref, grad_ref, up_ref, down_ref, out_ref):
        out_ref[0] = product(act_ref[...], down_ref[...], 1, 0).astype(BF)
        out_ref[1] = product(grad_ref[...], up_ref[...], 1, 1).astype(BF)

    whole = pl.BlockSpec((rows, units), lambda i: (0, 0))
    return local_kernel(
        body,
        (4,),
        [
            whole,
            whole,
            pl.BlockSpec((tile, units), lambda i: (i, 0)),
            pl.BlockSpec((units, tile), lambda i: (0, i)),
        ],
        pl.BlockSpec((2, rows, tile), lambda i: (0, 0, i)),
        jax.ShapeDtypeStruct((2, rows, features), BF),
        acts,
        grads,
        up,
        down,
    )


def weight_sums(sets, acts, grads, core):
    units = acts[0].shape[1] // 2
    features = sets[0].shape[2]
    tile = features // 4
    count = len(sets)

    def body(*refs):
        down_ref, up_ref = refs[-2:]
        down_sum = up_sum = None
        for i in range(count):
            down_part = product(refs[count + i][...], refs[i][1], 0, 0)
            up_part = product(refs[i][0], refs[2 * count + i][...], 0, 0)
            down_sum = down_part if i == 0 else down_sum + down_part
            up_sum = up_part if i == 0 else up_sum + up_part
        down_ref[...] = down_sum.astype(BF)
        up_ref[...] = up_sum.astype(BF)

    halves = [pl.BlockSpec((a.shape[0], units), lambda i: (0, core)) for a in acts]
    return local_kernel(
        body,
        (4,),
        [pl.BlockSpec((2, s.shape[1], tile), lambda i: (0, 0, i)) for s in sets] + halves + halves,
        [
            pl.BlockSpec((units, tile), lambda i: (0, i)),
            pl.BlockSpec((tile, units), lambda i: (i, 0)),
        ],
        [
            jax.ShapeDtypeStruct((units, features), BF),
            jax.ShapeDtypeStruct((features, units), BF),
        ],
        *sets,
        *acts,
        *grads,
    )


def along_x(value, hop):
    pairs = []
    for row in range(4):
        for core in range(2):
            to = (row + (hop if core == 0 else -hop)) % 4
            pairs.append((row * 2 + core, to * 2 + core))
    return lax.ppermute(value, ("row", "col"), pairs)


def across(value):
    return lax.ppermute(value, "col", [(0, 1), (1, 0)])


def plane(value, phase, hop):
    pairs = []
    for core in range(2):
        for z in range(4):
            for y in range(4):
                if core == phase:
                    to = ((z + hop) % 4) * 4 + y
                else:
                    to = z * 4 + (y + hop) % 4
                pairs.append((core * 16 + z * 4 + y, core * 16 + to))
    return lax.ppermute(value, ("col", "depth"), pairs)


def held(*values):
    return lax.optimization_barrier(values)


def on_device(tokens, up_weight, down_weight, out_grad):
    x = lax.axis_index("row")
    sign = 1 - 2 * lax.axis_index("col")
    rows, width = tokens.shape
    sub, half = rows // 4, rows // 2
    hid = up_weight.shape[1]

    turned = (0, 3, 2, 1)

    both = jnp.stack([tokens, out_grad]).reshape(2, 4, sub, width)

    def piece(k):
        return lax.dynamic_index_in_dim(both, (x + sign * k + 4) % 4, 1, keepdims=False)

    got = [piece(0)] + [along_x(piece(k), k) for k in (1, 2, 3)]
    own = jnp.stack(
        [
            jnp.concatenate([got[k][0] for k in range(4)], axis=1),
            jnp.concatenate([got[k][1] for k in turned], axis=1),
        ]
    )

    ups, downs = [up_weight], [down_weight]

    def step():
        ups.append(along_x(ups[-1], 1))
        downs.append(along_x(downs[-1], -1))

    def join(parts, axis):
        return jnp.concatenate(parts, axis=axis)

    def after(round_value):
        ups[-1], downs[-1], _ = held(ups[-1], downs[-1], round_value)

    step()
    after(own)
    step()
    first = join([own] + [plane(own, 0, hop) for hop in (1, 2, 3)], 1)
    after(first)

    up_early = across(join(ups[:2], 0))
    left, right = plane(first, 1, 1), plane(first, 1, -1)
    step()
    left, right, up_early, ups[3], downs[3] = held(left, right, up_early, ups[3], downs[3])
    (down_mine,) = held(join(downs, 1))
    up_late, down_theirs = across(join(ups[2:], 0)), across(down_mine)
    far = [plane(left[:, :half], 1, 1), plane(right[:, half:], 1, -1)]

    def rows_of(value, k):
        return lax.slice_in_dim(value, k * width, (k + 1) * width, axis=0)

    def columns(value, k):
        return lax.slice_in_dim(value, k * width, (k + 1) * width, axis=1)

    up = held(
        join(ups, 0),
        join([rows_of(up_early, 0), rows_of(up_late, 1), rows_of(up_late, 0), rows_of(up_early, 1)], 0),
    )
    down = held(down_mine, join([columns(down_theirs, k) for k in turned], 1))
    up, down = held(join(up, 1), join(down, 0))

    near = join([first, left, right], 1)
    near_acts, near_grads = forward(near, up, down)
    *far, near_acts, near_grads = held(*far, near_acts, near_grads)
    far = join(far, 1)
    far_acts, far_grads = forward(far, up, down)

    far_sums = backward(far_acts, far_grads, up, down)
    far_back = [far_sums[:, :half], far_sums[:, half:]]
    *far_back, near_acts, near_grads, far_acts, far_grads = held(
        *far_back, near_acts, near_grads, far_acts, far_grads
    )
    far_back = [plane(far_back[0], 1, -1), plane(far_back[1], 1, 1)]
    sets, acts, grads = (near, far), (near_acts, far_acts), (near_grads, far_grads)
    theirs = weight_sums(sets, acts, grads, 1)
    near_acts, near_grads, *theirs = held(near_acts, near_grads, *theirs)
    down_theirs, up_theirs = (across(value) for value in theirs)
    near_sums = backward(near_acts, near_grads, up, down)
    acts, grads = (near_acts, far_acts), (near_grads, far_grads)
    down_mine, up_mine = weight_sums(sets, acts, grads, 0)
    *far_back, near_sums, down_mine, up_mine, down_theirs, up_theirs = held(
        *far_back, near_sums, down_mine, up_mine, down_theirs, up_theirs
    )

    def total(*parts):
        value = parts[0].astype(F32)
        for part in parts[1:]:
            value = value + part.astype(F32)
        return value

    here, left, right = (near_sums[:, i * rows : (i + 1) * rows] for i in range(3))
    left = join([total(left[:, :half], far_back[0]).astype(BF), left[:, half:]], 1)
    right = join([right[:, :half], total(right[:, half:], far_back[1]).astype(BF)], 1)
    left, right = plane(left, 1, -1), plane(right, 1, 1)

    def down_part(k, *more):
        return total(columns(down_mine, k), columns(down_theirs, turned[k]), *more)

    def up_part(k, *more):
        return total(rows_of(up_mine, k), rows_of(up_theirs, turned[k]), *more)

    down_grad = along_x(down_part(1).astype(BF), -1)
    up_grad = along_x(up_part(1).astype(BF), 1)
    left, right, down_grad, up_grad = held(left, right, down_grad, up_grad)

    down_grad = along_x(down_part(2, down_grad).astype(BF), -1)
    up_grad = along_x(up_part(2, up_grad).astype(BF), 1)
    sums = total(here, left, right).astype(BF).reshape(2, 4, sub, 4 * width)
    end = total(sums[:, 0], *(plane(sums[:, hop], 0, -hop) for hop in (1, 2, 3))).astype(BF)
    down_grad, up_grad, _ = held(down_grad, up_grad, end)
    down_grad = along_x(down_part(3, down_grad).astype(BF), -1)
    up_grad = along_x(up_part(3, up_grad).astype(BF), 1)
    down_grad, up_grad = down_part(0, down_grad), up_part(0, up_grad)

    out = jnp.zeros((2, rows, width), BF)
    for k in range(4):
        sent = jnp.stack([columns(end[0], turned[k]), columns(end[1], k)])
        got = along_x(sent, -k) if k else sent
        at = (x + sign * k + 4) % 4 * sub
        out = lax.dynamic_update_slice_in_dim(out, got, at, axis=1)
    return out[0], out[1], up_grad, down_grad


def solution(mesh):
    spec = P(("col", "depth"), "row")
    wide = P("row", ("col", "depth"))
    return jax.shard_map(
        on_device,
        mesh=mesh,
        in_specs=(spec, wide, spec, spec),
        out_specs=(spec, spec, wide, spec),
        check_vma=False,
    )
```

```python
import jax
import jax.numpy as jnp
from jax import lax
from jax.experimental import pallas as pl
from jax.experimental.pallas import tpu as pltpu
from jax.sharding import PartitionSpec as P

BF = jnp.bfloat16
F32 = jnp.float32


def gelu_value(value):
    return value * 0.5 * (1.0 + lax.erf(value * 0.7071067811865476))


def gelu_slope(value):
    return (
        0.5 * (1.0 + lax.erf(value * 0.7071067811865476))
        + value * jnp.exp(-0.5 * value * value) * 0.3989422804014327
    )


def product(left, right, left_dim, right_dim):
    return lax.dot_general(
        left, right, (((left_dim,), (right_dim,)), ((), ())), preferred_element_type=F32
    )


def local_kernel(body, grid, in_specs, out_specs, out_shape, *arrays):
    return pl.pallas_call(
        body,
        grid=grid,
        in_specs=in_specs,
        out_specs=out_specs,
        out_shape=out_shape,
        compiler_params=pltpu.CompilerParams(vmem_limit_bytes=16 * 2**20),
        cost_estimate=pl.CostEstimate(flops=1, bytes_accessed=1, transcendentals=0),
    )(*arrays)


def forward(pair, up, down):
    _, rows, features = pair.shape
    units = up.shape[1]
    tile = units // 3

    def body(pair_ref, up_ref, down_ref, act_ref, grad_ref):
        hidden = product(pair_ref[0], up_ref[...], 1, 0)
        act_grad = product(pair_ref[1], down_ref[...], 1, 1)
        act_ref[...] = gelu_value(hidden).astype(BF)
        grad_ref[...] = (act_grad * gelu_slope(hidden)).astype(BF)

    out = pl.BlockSpec((rows, tile), lambda i: (0, i))
    shape = jax.ShapeDtypeStruct((rows, units), BF)
    return local_kernel(
        body,
        (3,),
        [
            pl.BlockSpec((2, rows, features), lambda i: (0, 0, 0), pipeline_mode=pl.Buffered(1)),
            pl.BlockSpec((features, tile), lambda i: (0, i)),
            pl.BlockSpec((tile, features), lambda i: (i, 0)),
        ],
        [out, out],
        [shape, shape],
        pair,
        up,
        down,
    )


def backward(acts, grads, up, down):
    rows, units = acts.shape
    features = up.shape[0]
    tile = features // 4

    def body(act_ref, grad_ref, up_ref, down_ref, out_ref):
        out_ref[0] = product(act_ref[...], down_ref[...], 1, 0).astype(BF)
        out_ref[1] = product(grad_ref[...], up_ref[...], 1, 1).astype(BF)

    whole = pl.BlockSpec((rows, units), lambda i: (0, 0))
    return local_kernel(
        body,
        (4,),
        [
            whole,
            whole,
            pl.BlockSpec((tile, units), lambda i: (i, 0)),
            pl.BlockSpec((units, tile), lambda i: (0, i)),
        ],
        pl.BlockSpec((2, rows, tile), lambda i: (0, 0, i)),
        jax.ShapeDtypeStruct((2, rows, features), BF),
        acts,
        grads,
        up,
        down,
    )


def weight_sums(sets, acts, grads, core):
    units = acts[0].shape[1] // 2
    features = sets[0].shape[2]
    tile = features // 4
    count = len(sets)

    def body(*refs):
        down_ref, up_ref = refs[-2:]
        down_sum = up_sum = None
        for i in range(count):
            down_part = product(refs[count + i][...], refs[i][1], 0, 0)
            up_part = product(refs[i][0], refs[2 * count + i][...], 0, 0)
            down_sum = down_part if i == 0 else down_sum + down_part
            up_sum = up_part if i == 0 else up_sum + up_part
        down_ref[0] = down_sum.astype(BF)
        up_ref[0] = up_sum.astype(BF)

    halves = [pl.BlockSpec((a.shape[0], units), lambda i: (0, core)) for a in acts]
    return local_kernel(
        body,
        (4,),
        [pl.BlockSpec((2, s.shape[1], tile), lambda i: (0, 0, i)) for s in sets] + halves + halves,
        [
            pl.BlockSpec((1, units, tile), lambda i: (i, 0, 0)),
            pl.BlockSpec((1, tile, units), lambda i: (i, 0, 0)),
        ],
        [
            jax.ShapeDtypeStruct((4, units, tile), BF),
            jax.ShapeDtypeStruct((4, tile, units), BF),
        ],
        *sets,
        *acts,
        *grads,
    )


def along_x(value, hop):
    pairs = []
    for row in range(4):
        for core in range(2):
            to = (row + (hop if core == 0 else -hop)) % 4
            pairs.append((row * 2 + core, to * 2 + core))
    return lax.ppermute(value, ("row", "col"), pairs)


def across(value):
    return lax.ppermute(value, "col", [(0, 1), (1, 0)])


def plane(value, phase, hop):
    pairs = []
    for core in range(2):
        for z in range(4):
            for y in range(4):
                if core == phase:
                    to = ((z + hop) % 4) * 4 + y
                else:
                    to = z * 4 + (y + hop) % 4
                pairs.append((core * 16 + z * 4 + y, core * 16 + to))
    return lax.ppermute(value, ("col", "depth"), pairs)


def held(*values):
    return lax.optimization_barrier(values)


def on_device(tokens, up_weight, down_weight, out_grad):
    x = lax.axis_index("row")
    sign = 1 - 2 * lax.axis_index("col")
    rows, width = tokens.shape
    sub, half = rows // 4, rows // 2
    hid = up_weight.shape[1]

    turned = (0, 3, 2, 1)

    both = jnp.stack([tokens, out_grad]).reshape(2, 4, sub, width)

    def piece(k):
        return lax.dynamic_index_in_dim(both, (x + sign * k + 4) % 4, 1, keepdims=False)

    got = [piece(0)] + [along_x(piece(k), k) for k in (1, 2, 3)]
    own = jnp.stack(
        [
            jnp.concatenate([got[k][0] for k in range(4)], axis=1),
            jnp.concatenate([got[k][1] for k in turned], axis=1),
        ]
    )

    ups, downs = [up_weight], [down_weight]

    def step():
        ups.append(along_x(ups[-1], 1))
        downs.append(along_x(downs[-1], -1))

    def join(parts, axis):
        return jnp.concatenate(parts, axis=axis)

    def after(round_value):
        ups[-1], downs[-1], _ = held(ups[-1], downs[-1], round_value)

    step()
    after(own)
    step()
    first = join([own] + [plane(own, 0, hop) for hop in (1, 2, 3)], 1)
    after(first)

    up_early = across(join(ups[:2], 0))
    left, right = plane(first, 1, 1), plane(first, 1, -1)
    step()
    up_last, down_last = across(ups[3]), across(downs[3])
    left, right, up_early, up_last, down_last, ups[3], downs[3] = held(
        left, right, up_early, up_last, down_last, ups[3], downs[3]
    )
    far = [plane(left[:, :half], 1, 1), plane(right[:, half:], 1, -1)]
    up_other, down_early = across(ups[2]), across(join(downs[:3], 1))

    def rows_of(value, k):
        return lax.slice_in_dim(value, k * width, (k + 1) * width, axis=0)

    def columns(value, k):
        return lax.slice_in_dim(value, k * width, (k + 1) * width, axis=1)

    up = held(join(ups, 0), join([rows_of(up_early, 0), up_last, up_other, rows_of(up_early, 1)], 0))
    down = held(
        join(downs, 1),
        join([columns(down_early, 0), down_last, columns(down_early, 2), columns(down_early, 1)], 1),
    )
    up, down = held(join(up, 1), join(down, 0))

    near = join([first, left, right], 1)
    near_acts, near_grads = forward(near, up, down)
    *far, near_acts, near_grads = held(*far, near_acts, near_grads)
    far = join(far, 1)
    far_acts, far_grads = forward(far, up, down)

    far_sums = backward(far_acts, far_grads, up, down)
    far_back = [far_sums[:, :half], far_sums[:, half:]]
    *far_back, near_acts, near_grads, far_acts, far_grads = held(
        *far_back, near_acts, near_grads, far_acts, far_grads
    )
    far_back = [plane(far_back[0], 1, -1), plane(far_back[1], 1, 1)]
    near_sums = backward(near_acts, near_grads, up, down)
    near_acts, near_grads, near_sums = held(near_acts, near_grads, near_sums)
    sets, acts, grads = (near, far), (near_acts, far_acts), (near_grads, far_grads)
    theirs = weight_sums(sets, acts, grads, 1)
    *far_back, near_sums, down_other, up_other = held(*far_back, near_sums, *theirs)
    mine = weight_sums(sets, acts, grads, 0)

    def total(*parts):
        value = parts[0].astype(F32)
        for part in parts[1:]:
            value = value + part.astype(F32)
        return value

    here, left, right = (near_sums[:, i * rows : (i + 1) * rows] for i in range(3))
    left = join([total(left[:, :half], far_back[0]).astype(BF), left[:, half:]], 1)
    right = join([right[:, :half], total(right[:, half:], far_back[1]).astype(BF)], 1)
    left, right = plane(left, 1, -1), plane(right, 1, 1)

    def swap(k, round_value):
        down_sum, up_sum, _ = held(down_other[turned[k]], up_other[turned[k]], round_value)
        return across(down_sum), across(up_sum)

    down_theirs, up_theirs = swap(1, near_sums)
    down_grad = along_x(total(mine[0][1], down_theirs).astype(BF), -1)
    up_grad = along_x(total(mine[1][1], up_theirs).astype(BF), 1)

    left, right, down_grad, up_grad = held(left, right, down_grad, up_grad)

    down_theirs, up_theirs = swap(2, left)
    down_grad = along_x(total(mine[0][2], down_theirs, down_grad).astype(BF), -1)
    up_grad = along_x(total(mine[1][2], up_theirs, up_grad).astype(BF), 1)
    sums = total(here, left, right).astype(BF).reshape(2, 4, sub, 4 * width)
    end = total(sums[:, 0], *(plane(sums[:, hop], 0, -hop) for hop in (1, 2, 3))).astype(BF)

    end, down_grad, up_grad = held(end, down_grad, up_grad)

    down_theirs, up_theirs = swap(3, end)
    down_grad = along_x(total(mine[0][3], down_theirs, down_grad).astype(BF), -1)
    up_grad = along_x(total(mine[1][3], up_theirs, up_grad).astype(BF), 1)
    down_theirs, up_theirs = swap(0, end)
    down_grad = total(mine[0][0], down_theirs, down_grad)
    up_grad = total(mine[1][0], up_theirs, up_grad)

    out = jnp.zeros((2, rows, width), BF)
    for k in range(4):
        sent = jnp.stack([columns(end[0], turned[k]), columns(end[1], k)])
        got = along_x(sent, -k) if k else sent
        at = (x + sign * k + 4) % 4 * sub
        out = lax.dynamic_update_slice_in_dim(out, got, at, axis=1)
    return out[0], out[1], up_grad, down_grad


def solution(mesh):
    spec = P(("col", "depth"), "row")
    wide = P("row", ("col", "depth"))
    return jax.shard_map(
        on_device,
        mesh=mesh,
        in_specs=(spec, wide, spec, spec),
        out_specs=(spec, spec, wide, spec),
        check_vma=False,
    )
```

```python
import jax
import jax.numpy as jnp
from jax import lax
from jax.experimental import pallas as pl
from jax.experimental.pallas import tpu as pltpu
from jax.sharding import PartitionSpec as P

BF = jnp.bfloat16
F32 = jnp.float32


def gelu_value(value):
    return value * 0.5 * (1.0 + lax.erf(value * 0.7071067811865476))


def gelu_slope(value):
    return (
        0.5 * (1.0 + lax.erf(value * 0.7071067811865476))
        + value * jnp.exp(-0.5 * value * value) * 0.3989422804014327
    )


def product(left, right, left_dim, right_dim):
    return lax.dot_general(
        left, right, (((left_dim,), (right_dim,)), ((), ())), preferred_element_type=F32
    )


def local_kernel(body, grid, in_specs, out_specs, out_shape, *arrays):
    return pl.pallas_call(
        body,
        grid=grid,
        in_specs=in_specs,
        out_specs=out_specs,
        out_shape=out_shape,
        compiler_params=pltpu.CompilerParams(vmem_limit_bytes=16 * 2**20),
        cost_estimate=pl.CostEstimate(flops=1, bytes_accessed=1, transcendentals=0),
    )(*arrays)


def forward(pair, up, down):
    _, rows, features = pair.shape
    units = up.shape[1]
    tile = units // 3

    def body(pair_ref, up_ref, down_ref, act_ref, grad_ref):
        hidden = product(pair_ref[0], up_ref[...], 1, 0)
        act_grad = product(pair_ref[1], down_ref[...], 1, 1)
        act_ref[...] = gelu_value(hidden).astype(BF)
        grad_ref[...] = (act_grad * gelu_slope(hidden)).astype(BF)

    out = pl.BlockSpec((rows, tile), lambda i: (0, i))
    shape = jax.ShapeDtypeStruct((rows, units), BF)
    return local_kernel(
        body,
        (3,),
        [
            pl.BlockSpec((2, rows, features), lambda i: (0, 0, 0), pipeline_mode=pl.Buffered(1)),
            pl.BlockSpec((features, tile), lambda i: (0, i)),
            pl.BlockSpec((tile, features), lambda i: (i, 0)),
        ],
        [out, out],
        [shape, shape],
        pair,
        up,
        down,
    )


def backward(acts, grads, up, down):
    rows, units = acts.shape
    features = up.shape[0]
    tile = features // 4

    def body(act_ref, grad_ref, up_ref, down_ref, out_ref):
        out_ref[0] = product(act_ref[...], down_ref[...], 1, 0).astype(BF)
        out_ref[1] = product(grad_ref[...], up_ref[...], 1, 1).astype(BF)

    whole = pl.BlockSpec((rows, units), lambda i: (0, 0))
    return local_kernel(
        body,
        (4,),
        [
            whole,
            whole,
            pl.BlockSpec((tile, units), lambda i: (i, 0)),
            pl.BlockSpec((units, tile), lambda i: (0, i)),
        ],
        pl.BlockSpec((2, rows, tile), lambda i: (0, 0, i)),
        jax.ShapeDtypeStruct((2, rows, features), BF),
        acts,
        grads,
        up,
        down,
    )


def weight_sums(sets, acts, grads, core):
    units = acts[0].shape[1] // 2
    features = sets[0].shape[2]
    tile = features // 4
    count = len(sets)

    def body(*refs):
        down_ref, up_ref = refs[-2:]
        down_sum = up_sum = None
        for i in range(count):
            down_part = product(refs[count + i][...], refs[i][1], 0, 0)
            up_part = product(refs[i][0], refs[2 * count + i][...], 0, 0)
            down_sum = down_part if i == 0 else down_sum + down_part
            up_sum = up_part if i == 0 else up_sum + up_part
        down_ref[0] = down_sum.astype(BF)
        up_ref[0] = up_sum.astype(BF)

    halves = [pl.BlockSpec((a.shape[0], units), lambda i: (0, core)) for a in acts]
    return local_kernel(
        body,
        (4,),
        [pl.BlockSpec((2, s.shape[1], tile), lambda i: (0, 0, i)) for s in sets] + halves + halves,
        [
            pl.BlockSpec((1, units, tile), lambda i: (i, 0, 0)),
            pl.BlockSpec((1, tile, units), lambda i: (i, 0, 0)),
        ],
        [
            jax.ShapeDtypeStruct((4, units, tile), BF),
            jax.ShapeDtypeStruct((4, tile, units), BF),
        ],
        *sets,
        *acts,
        *grads,
    )


def along_x(value, hop):
    pairs = []
    for row in range(4):
        for core in range(2):
            to = (row + (hop if core == 0 else -hop)) % 4
            pairs.append((row * 2 + core, to * 2 + core))
    return lax.ppermute(value, ("row", "col"), pairs)


def across(value):
    return lax.ppermute(value, "col", [(0, 1), (1, 0)])


def plane(value, phase, hop):
    pairs = []
    for core in range(2):
        for z in range(4):
            for y in range(4):
                if core == phase:
                    to = ((z + hop) % 4) * 4 + y
                else:
                    to = z * 4 + (y + hop) % 4
                pairs.append((core * 16 + z * 4 + y, core * 16 + to))
    return lax.ppermute(value, ("col", "depth"), pairs)


def held(*values):
    return lax.optimization_barrier(values)


def on_device(tokens, up_weight, down_weight, out_grad):
    x = lax.axis_index("row")
    sign = 1 - 2 * lax.axis_index("col")
    rows, width = tokens.shape
    sub, half = rows // 4, rows // 2
    hid = up_weight.shape[1]

    turned = (0, 3, 2, 1)

    both = jnp.stack([tokens, out_grad]).reshape(2, 4, sub, width)

    def piece(k):
        return lax.dynamic_index_in_dim(both, (x + sign * k + 4) % 4, 1, keepdims=False)

    got = [piece(0)] + [along_x(piece(k), k) for k in (1, 2, 3)]
    own = jnp.stack(
        [
            jnp.concatenate([got[k][0] for k in range(4)], axis=1),
            jnp.concatenate([got[k][1] for k in turned], axis=1),
        ]
    )

    ups, downs = [up_weight], [down_weight]

    def step():
        ups.append(along_x(ups[-1], 1))
        downs.append(along_x(downs[-1], -1))

    def join(parts, axis):
        return jnp.concatenate(parts, axis=axis)

    def after(round_value):
        ups[-1], downs[-1], _ = held(ups[-1], downs[-1], round_value)

    step()
    after(own)
    step()
    first = join([own] + [plane(own, 0, hop) for hop in (1, 2, 3)], 1)
    after(first)

    up_early = across(join(ups[:2], 0))
    left, right = plane(first, 1, 1), plane(first, 1, -1)
    step()
    up_last, down_last = across(ups[3]), across(downs[3])
    left, right, up_early, up_last, down_last, ups[3], downs[3] = held(
        left, right, up_early, up_last, down_last, ups[3], downs[3]
    )
    far = [plane(left[:, :half], 1, 1), plane(right[:, half:], 1, -1)]
    up_other, down_early = across(ups[2]), across(join(downs[:3], 1))

    def rows_of(value, k):
        return lax.slice_in_dim(value, k * width, (k + 1) * width, axis=0)

    def columns(value, k):
        return lax.slice_in_dim(value, k * width, (k + 1) * width, axis=1)

    up = held(join(ups, 0), join([rows_of(up_early, 0), up_last, up_other, rows_of(up_early, 1)], 0))
    down = held(
        join(downs, 1),
        join([columns(down_early, 0), down_last, columns(down_early, 2), columns(down_early, 1)], 1),
    )
    up, down = held(join(up, 1), join(down, 0))

    near = join([first, left, right], 1)
    near_acts, near_grads = forward(near, up, down)
    *far, near_acts, near_grads = held(*far, near_acts, near_grads)
    far = join(far, 1)
    far_acts, far_grads = forward(far, up, down)

    far_sums = backward(far_acts, far_grads, up, down)
    far_back = [far_sums[:, :half], far_sums[:, half:]]
    *far_back, near_acts, near_grads, far_acts, far_grads = held(
        *far_back, near_acts, near_grads, far_acts, far_grads
    )
    far_back = [plane(far_back[0], 1, -1), plane(far_back[1], 1, 1)]
    near_sums = backward(near_acts, near_grads, up, down)
    near_acts, near_grads, near_sums = held(near_acts, near_grads, near_sums)
    sets, acts, grads = (near, far), (near_acts, far_acts), (near_grads, far_grads)
    theirs = weight_sums(sets, acts, grads, 1)
    *far_back, near_sums, down_other, up_other = held(*far_back, near_sums, *theirs)
    mine = weight_sums(sets, acts, grads, 0)

    def total(*parts):
        value = parts[0].astype(F32)
        for part in parts[1:]:
            value = value + part.astype(F32)
        return value

    here, left, right = (near_sums[:, i * rows : (i + 1) * rows] for i in range(3))
    left = join([total(left[:, :half], far_back[0]).astype(BF), left[:, half:]], 1)
    right = join([right[:, :half], total(right[:, half:], far_back[1]).astype(BF)], 1)
    near_sent = (left, right)
    left, right = plane(left, 1, -1), plane(right, 1, 1)

    def swap(blocks, round_value):
        down_sum, up_sum, _ = held(down_other[blocks], up_other[blocks], round_value)
        return across(down_sum), across(up_sum)

    down_theirs, up_theirs = swap(3, near_sent)
    down_grad = along_x(total(mine[0][1], down_theirs).astype(BF), -1)
    up_grad = along_x(total(mine[1][1], up_theirs).astype(BF), 1)
    left, right, down_grad, up_grad = held(left, right, down_grad, up_grad)

    down_theirs, up_theirs = swap(slice(0, 3), left)
    down_grad = along_x(total(mine[0][2], down_theirs[2], down_grad).astype(BF), -1)
    up_grad = along_x(total(mine[1][2], up_theirs[2], up_grad).astype(BF), 1)
    sums = total(here, left, right).astype(BF).reshape(2, 4, sub, 4 * width)
    end = total(sums[:, 0], *(plane(sums[:, hop], 0, -hop) for hop in (1, 2, 3))).astype(BF)
    end, down_grad, up_grad = held(end, down_grad, up_grad)

    down_grad = along_x(total(mine[0][3], down_theirs[1], down_grad).astype(BF), -1)
    up_grad = along_x(total(mine[1][3], up_theirs[1], up_grad).astype(BF), 1)

    out = jnp.zeros((2, rows, width), BF)
    for k in range(4):
        sent = jnp.stack([columns(end[0], turned[k]), columns(end[1], k)])
        got = along_x(sent, -k) if k else sent
        at = (x + sign * k + 4) % 4 * sub
        out = lax.dynamic_update_slice_in_dim(out, got, at, axis=1)
    down_grad = total(mine[0][0], down_theirs[0], down_grad)
    up_grad = total(mine[1][0], up_theirs[0], up_grad)
    return out[0], out[1], up_grad, down_grad


def solution(mesh):
    spec = P(("col", "depth"), "row")
    wide = P("row", ("col", "depth"))
    return jax.shard_map(
        on_device,
        mesh=mesh,
        in_specs=(spec, wide, spec, spec),
        out_specs=(spec, spec, wide, spec),
        check_vma=False,
    )
```

```python
import jax
import jax.numpy as jnp
from jax import lax
from jax.experimental import pallas as pl
from jax.experimental.pallas import tpu as pltpu
from jax.sharding import PartitionSpec as P

BF = jnp.bfloat16
F32 = jnp.float32


def gelu_value(value):
    return value * 0.5 * (1.0 + lax.erf(value * 0.7071067811865476))


def gelu_slope(value):
    return (
        0.5 * (1.0 + lax.erf(value * 0.7071067811865476))
        + value * jnp.exp(-0.5 * value * value) * 0.3989422804014327
    )


def product(left, right, left_dim, right_dim):
    return lax.dot_general(
        left, right, (((left_dim,), (right_dim,)), ((), ())), preferred_element_type=F32
    )


def local_kernel(body, grid, in_specs, out_specs, out_shape, *arrays):
    return pl.pallas_call(
        body,
        grid=grid,
        in_specs=in_specs,
        out_specs=out_specs,
        out_shape=out_shape,
        compiler_params=pltpu.CompilerParams(vmem_limit_bytes=16 * 2**20),
        cost_estimate=pl.CostEstimate(flops=1, bytes_accessed=1, transcendentals=0),
    )(*arrays)


def forward(pair, up, down):
    _, rows, features = pair.shape
    units = up.shape[1]
    tile = units // 3

    def body(pair_ref, up_ref, down_ref, act_ref, grad_ref):
        hidden = product(pair_ref[0], up_ref[...], 1, 0)
        act_grad = product(pair_ref[1], down_ref[...], 1, 1)
        act_ref[...] = gelu_value(hidden).astype(BF)
        grad_ref[...] = (act_grad * gelu_slope(hidden)).astype(BF)

    out = pl.BlockSpec((rows, tile), lambda i: (0, i))
    shape = jax.ShapeDtypeStruct((rows, units), BF)
    return local_kernel(
        body,
        (3,),
        [
            pl.BlockSpec((2, rows, features), lambda i: (0, 0, 0), pipeline_mode=pl.Buffered(1)),
            pl.BlockSpec((features, tile), lambda i: (0, i)),
            pl.BlockSpec((tile, features), lambda i: (i, 0)),
        ],
        [out, out],
        [shape, shape],
        pair,
        up,
        down,
    )


def backward(acts, grads, up, down):
    rows, units = acts.shape
    features = up.shape[0]
    tile = features // 4

    def body(act_ref, grad_ref, up_ref, down_ref, out_ref):
        out_ref[0] = product(act_ref[...], down_ref[...], 1, 0).astype(BF)
        out_ref[1] = product(grad_ref[...], up_ref[...], 1, 1).astype(BF)

    whole = pl.BlockSpec((rows, units), lambda i: (0, 0))
    return local_kernel(
        body,
        (4,),
        [
            whole,
            whole,
            pl.BlockSpec((tile, units), lambda i: (i, 0)),
            pl.BlockSpec((units, tile), lambda i: (0, i)),
        ],
        pl.BlockSpec((2, rows, tile), lambda i: (0, 0, i)),
        jax.ShapeDtypeStruct((2, rows, features), BF),
        acts,
        grads,
        up,
        down,
    )


def weight_sums(sets, acts, grads, core, apart):
    units = acts[0].shape[1] // 2
    features = sets[0].shape[2]
    tile = features // 4
    count = len(sets)
    joint = 3 if apart else 4

    def body(*refs):
        outs = refs[3 * count :]
        down_sum = up_sum = None
        for i in range(count):
            down_part = product(refs[count + i][...], refs[i][1], 0, 0)
            up_part = product(refs[i][0], refs[2 * count + i][...], 0, 0)
            down_sum = down_part if i == 0 else down_sum + down_part
            up_sum = up_part if i == 0 else up_sum + up_part

        @pl.when(pl.program_id(0) < joint)
        def _():
            outs[0][0] = down_sum.astype(BF)
            outs[1][0] = up_sum.astype(BF)

        if apart:

            @pl.when(pl.program_id(0) == joint)
            def _():
                outs[2][...] = down_sum.astype(BF)
                outs[3][...] = up_sum.astype(BF)

    halves = [pl.BlockSpec((a.shape[0], units), lambda i: (0, core)) for a in acts]
    out_specs = [
        pl.BlockSpec((1, units, tile), lambda i: (jnp.minimum(i, joint - 1), 0, 0)),
        pl.BlockSpec((1, tile, units), lambda i: (jnp.minimum(i, joint - 1), 0, 0)),
    ]
    out_shape = [
        jax.ShapeDtypeStruct((joint, units, tile), BF),
        jax.ShapeDtypeStruct((joint, tile, units), BF),
    ]
    if apart:
        out_specs += [
            pl.BlockSpec((units, tile), lambda i: (0, 0)),
            pl.BlockSpec((tile, units), lambda i: (0, 0)),
        ]
        out_shape += [
            jax.ShapeDtypeStruct((units, tile), BF),
            jax.ShapeDtypeStruct((tile, units), BF),
        ]
    return local_kernel(
        body,
        (4,),
        [pl.BlockSpec((2, s.shape[1], tile), lambda i: (0, 0, i)) for s in sets] + halves + halves,
        out_specs,
        out_shape,
        *sets,
        *acts,
        *grads,
    )


def along_x(value, hop):
    pairs = []
    for row in range(4):
        for core in range(2):
            to = (row + (hop if core == 0 else -hop)) % 4
            pairs.append((row * 2 + core, to * 2 + core))
    return lax.ppermute(value, ("row", "col"), pairs)


def across(value):
    return lax.ppermute(value, "col", [(0, 1), (1, 0)])


def plane(value, phase, hop):
    pairs = []
    for core in range(2):
        for z in range(4):
            for y in range(4):
                if core == phase:
                    to = ((z + hop) % 4) * 4 + y
                else:
                    to = z * 4 + (y + hop) % 4
                pairs.append((core * 16 + z * 4 + y, core * 16 + to))
    return lax.ppermute(value, ("col", "depth"), pairs)


def held(*values):
    return lax.optimization_barrier(values)


def on_device(tokens, up_weight, down_weight, out_grad):
    x = lax.axis_index("row")
    sign = 1 - 2 * lax.axis_index("col")
    rows, width = tokens.shape
    sub, half = rows // 4, rows // 2
    hid = up_weight.shape[1]

    turned = (0, 3, 2, 1)

    both = jnp.stack([tokens, out_grad]).reshape(2, 4, sub, width)

    def piece(k):
        return lax.dynamic_index_in_dim(both, (x + sign * k + 4) % 4, 1, keepdims=False)

    got = [piece(0)] + [along_x(piece(k), k) for k in (1, 2, 3)]
    own = jnp.stack(
        [
            jnp.concatenate([got[k][0] for k in range(4)], axis=1),
            jnp.concatenate([got[k][1] for k in turned], axis=1),
        ]
    )

    ups, downs = [up_weight], [down_weight]

    def step():
        ups.append(along_x(ups[-1], 1))
        downs.append(along_x(downs[-1], -1))

    def join(parts, axis):
        return jnp.concatenate(parts, axis=axis)

    def after(round_value):
        ups[-1], downs[-1], _ = held(ups[-1], downs[-1], round_value)

    step()
    after(own)
    step()
    first = join([own] + [plane(own, 0, hop) for hop in (1, 2, 3)], 1)
    after(first)

    up_early = across(join(ups[:2], 0))
    left, right = plane(first, 1, 1), plane(first, 1, -1)
    step()
    up_last, down_last = across(ups[3]), across(downs[3])
    left, right, up_early, up_last, down_last, ups[3], downs[3] = held(
        left, right, up_early, up_last, down_last, ups[3], downs[3]
    )
    far = [plane(left[:, :half], 1, 1), plane(right[:, half:], 1, -1)]
    up_other, down_early = across(ups[2]), across(join(downs[:3], 1))

    def rows_of(value, k):
        return lax.slice_in_dim(value, k * width, (k + 1) * width, axis=0)

    def columns(value, k):
        return lax.slice_in_dim(value, k * width, (k + 1) * width, axis=1)

    up = held(join(ups, 0), join([rows_of(up_early, 0), up_last, up_other, rows_of(up_early, 1)], 0))
    down = held(
        join(downs, 1),
        join([columns(down_early, 0), down_last, columns(down_early, 2), columns(down_early, 1)], 1),
    )
    up, down = held(join(up, 1), join(down, 0))

    near = join([first, left, right], 1)
    near_acts, near_grads = forward(near, up, down)
    *far, near_acts, near_grads = held(*far, near_acts, near_grads)
    far = join(far, 1)
    far_acts, far_grads = forward(far, up, down)

    far_sums = backward(far_acts, far_grads, up, down)
    far_back = [far_sums[:, :half], far_sums[:, half:]]
    *far_back, near_acts, near_grads, far_acts, far_grads = held(
        *far_back, near_acts, near_grads, far_acts, far_grads
    )
    far_back = [plane(far_back[0], 1, -1), plane(far_back[1], 1, 1)]
    near_sums = backward(near_acts, near_grads, up, down)
    near_acts, near_grads, near_sums = held(near_acts, near_grads, near_sums)
    sets, acts, grads = (near, far), (near_acts, far_acts), (near_grads, far_grads)
    theirs = weight_sums(sets, acts, grads, 1, True)
    far_back[0], far_back[1], near_sums, *theirs = held(*far_back, near_sums, *theirs)
    mine = weight_sums(sets, acts, grads, 0, False)

    def total(*parts):
        value = parts[0].astype(F32)
        for part in parts[1:]:
            value = value + part.astype(F32)
        return value

    here, left, right = (near_sums[:, i * rows : (i + 1) * rows] for i in range(3))
    left = join([total(left[:, :half], far_back[0]).astype(BF), left[:, half:]], 1)
    right = join([right[:, :half], total(right[:, half:], far_back[1]).astype(BF)], 1)
    near_sent = (left, right)
    left, right = plane(left, 1, -1), plane(right, 1, 1)

    def swap(pair, round_value):
        down_sum, up_sum, _ = held(*pair, round_value)
        return across(down_sum), across(up_sum)

    down_theirs, up_theirs = swap(theirs[2:], near_sent)
    down_grad = along_x(total(mine[0][1], down_theirs).astype(BF), -1)
    up_grad = along_x(total(mine[1][1], up_theirs).astype(BF), 1)
    left, right, down_grad, up_grad = held(left, right, down_grad, up_grad)

    down_theirs, up_theirs = swap(theirs[:2], left)
    down_grad = along_x(total(mine[0][2], down_theirs[2], down_grad).astype(BF), -1)
    up_grad = along_x(total(mine[1][2], up_theirs[2], up_grad).astype(BF), 1)
    sums = total(here, left, right).astype(BF).reshape(2, 4, sub, 4 * width)
    end = total(sums[:, 0], *(plane(sums[:, hop], 0, -hop) for hop in (1, 2, 3))).astype(BF)
    end, down_grad, up_grad = held(end, down_grad, up_grad)

    down_grad = along_x(total(mine[0][3], down_theirs[1], down_grad).astype(BF), -1)
    up_grad = along_x(total(mine[1][3], up_theirs[1], up_grad).astype(BF), 1)

    out = jnp.zeros((2, rows, width), BF)
    for k in range(4):
        sent = jnp.stack([columns(end[0], turned[k]), columns(end[1], k)])
        got = along_x(sent, -k) if k else sent
        at = (x + sign * k + 4) % 4 * sub
        out = lax.dynamic_update_slice_in_dim(out, got, at, axis=1)
    down_grad = total(mine[0][0], down_theirs[0], down_grad)
    up_grad = total(mine[1][0], up_theirs[0], up_grad)
    return out[0], out[1], up_grad, down_grad


def solution(mesh):
    spec = P(("col", "depth"), "row")
    wide = P("row", ("col", "depth"))
    return jax.shard_map(
        on_device,
        mesh=mesh,
        in_specs=(spec, wide, spec, spec),
        out_specs=(spec, spec, wide, spec),
        check_vma=False,
    )
```

```python
import jax
import jax.numpy as jnp
from jax import lax
from jax.experimental import pallas as pl
from jax.experimental.pallas import tpu as pltpu
from jax.sharding import PartitionSpec as P

BF = jnp.bfloat16
F32 = jnp.float32


def gelu_value(value):
    return value * 0.5 * (1.0 + lax.erf(value * 0.7071067811865476))


def gelu_slope(value):
    return (
        0.5 * (1.0 + lax.erf(value * 0.7071067811865476))
        + value * jnp.exp(-0.5 * value * value) * 0.3989422804014327
    )


def product(left, right, left_dim, right_dim):
    return lax.dot_general(
        left, right, (((left_dim,), (right_dim,)), ((), ())), preferred_element_type=F32
    )


def local_kernel(body, grid, in_specs, out_specs, out_shape, *arrays):
    return pl.pallas_call(
        body,
        grid=grid,
        in_specs=in_specs,
        out_specs=out_specs,
        out_shape=out_shape,
        compiler_params=pltpu.CompilerParams(vmem_limit_bytes=16 * 2**20),
        cost_estimate=pl.CostEstimate(flops=1, bytes_accessed=1, transcendentals=0),
    )(*arrays)


def forward(pair, up, down):
    _, rows, features = pair.shape
    units = up.shape[1]
    tile = units // 3

    def body(pair_ref, up_ref, down_ref, act_ref, grad_ref):
        hidden = product(pair_ref[0], up_ref[...], 1, 0)
        act_grad = product(pair_ref[1], down_ref[...], 1, 1)
        act_ref[...] = gelu_value(hidden).astype(BF)
        grad_ref[...] = (act_grad * gelu_slope(hidden)).astype(BF)

    out = pl.BlockSpec((rows, tile), lambda i: (0, i))
    shape = jax.ShapeDtypeStruct((rows, units), BF)
    return local_kernel(
        body,
        (3,),
        [
            pl.BlockSpec((2, rows, features), lambda i: (0, 0, 0), pipeline_mode=pl.Buffered(1)),
            pl.BlockSpec((features, tile), lambda i: (0, i)),
            pl.BlockSpec((tile, features), lambda i: (i, 0)),
        ],
        [out, out],
        [shape, shape],
        pair,
        up,
        down,
    )


def backward(acts, grads, up, down):
    rows, units = acts.shape
    features = up.shape[0]
    tile = features // 4

    def body(act_ref, grad_ref, up_ref, down_ref, out_ref):
        out_ref[0] = product(act_ref[...], down_ref[...], 1, 0).astype(BF)
        out_ref[1] = product(grad_ref[...], up_ref[...], 1, 1).astype(BF)

    whole = pl.BlockSpec((rows, units), lambda i: (0, 0))
    return local_kernel(
        body,
        (4,),
        [
            whole,
            whole,
            pl.BlockSpec((tile, units), lambda i: (i, 0)),
            pl.BlockSpec((units, tile), lambda i: (0, i)),
        ],
        pl.BlockSpec((2, rows, tile), lambda i: (0, 0, i)),
        jax.ShapeDtypeStruct((2, rows, features), BF),
        acts,
        grads,
        up,
        down,
    )


def weight_sums(sets, acts, grads, core):
    units = acts[0].shape[1] // 2
    features = sets[0].shape[2]
    tile = features // 4
    count = len(sets)

    def body(*refs):
        down_ref, up_ref = refs[-2:]
        down_sum = up_sum = None
        for i in range(count):
            down_part = product(refs[count + i][...], refs[i][1], 0, 0)
            up_part = product(refs[i][0], refs[2 * count + i][...], 0, 0)
            down_sum = down_part if i == 0 else down_sum + down_part
            up_sum = up_part if i == 0 else up_sum + up_part
        down_ref[0] = down_sum.astype(BF)
        up_ref[0] = up_sum.astype(BF)

    halves = [pl.BlockSpec((a.shape[0], units), lambda i: (0, core)) for a in acts]
    return local_kernel(
        body,
        (4,),
        [pl.BlockSpec((2, s.shape[1], tile), lambda i: (0, 0, i)) for s in sets] + halves + halves,
        [
            pl.BlockSpec((1, units, tile), lambda i: (i, 0, 0)),
            pl.BlockSpec((1, tile, units), lambda i: (i, 0, 0)),
        ],
        [
            jax.ShapeDtypeStruct((4, units, tile), BF),
            jax.ShapeDtypeStruct((4, tile, units), BF),
        ],
        *sets,
        *acts,
        *grads,
    )


def along_x(value, hop):
    pairs = []
    for row in range(4):
        for core in range(2):
            to = (row + (hop if core == 0 else -hop)) % 4
            pairs.append((row * 2 + core, to * 2 + core))
    return lax.ppermute(value, ("row", "col"), pairs)


def across(value):
    return lax.ppermute(value, "col", [(0, 1), (1, 0)])


def plane(value, phase, hop):
    pairs = []
    for core in range(2):
        for z in range(4):
            for y in range(4):
                if core == phase:
                    to = ((z + hop) % 4) * 4 + y
                else:
                    to = z * 4 + (y + hop) % 4
                pairs.append((core * 16 + z * 4 + y, core * 16 + to))
    return lax.ppermute(value, ("col", "depth"), pairs)


def held(*values):
    return lax.optimization_barrier(values)


def on_device(tokens, up_weight, down_weight, out_grad):
    x = lax.axis_index("row")
    sign = 1 - 2 * lax.axis_index("col")
    rows, width = tokens.shape
    sub, half = rows // 4, rows // 2
    hid = up_weight.shape[1]

    turned = (0, 3, 2, 1)

    both = jnp.stack([tokens, out_grad]).reshape(2, 4, sub, width)

    def piece(k):
        return lax.dynamic_index_in_dim(both, (x + sign * k + 4) % 4, 1, keepdims=False)

    got = [piece(0)] + [along_x(piece(k), k) for k in (1, 2, 3)]
    own = jnp.stack(
        [
            jnp.concatenate([got[k][0] for k in range(4)], axis=1),
            jnp.concatenate([got[k][1] for k in turned], axis=1),
        ]
    )

    ups, downs = [up_weight], [down_weight]

    def step():
        ups.append(along_x(ups[-1], 1))
        downs.append(along_x(downs[-1], -1))

    def join(parts, axis):
        return jnp.concatenate(parts, axis=axis)

    def after(round_value):
        ups[-1], downs[-1], _ = held(ups[-1], downs[-1], round_value)

    step()
    after(own)
    step()
    first = join([own] + [plane(own, 0, hop) for hop in (1, 2, 3)], 1)
    after(first)

    up_early = across(join(ups[:2], 0))
    left, right = plane(first, 1, 1), plane(first, 1, -1)
    step()
    up_last, down_last = across(ups[3]), across(downs[3])
    left, right, up_early, up_last, down_last, ups[3], downs[3] = held(
        left, right, up_early, up_last, down_last, ups[3], downs[3]
    )
    far = [plane(left[:, :half], 1, 1), plane(right[:, half:], 1, -1)]
    up_other, down_early = across(ups[2]), across(join(downs[:3], 1))

    def rows_of(value, k):
        return lax.slice_in_dim(value, k * width, (k + 1) * width, axis=0)

    def columns(value, k):
        return lax.slice_in_dim(value, k * width, (k + 1) * width, axis=1)

    up = held(join(ups, 0), join([rows_of(up_early, 0), up_last, up_other, rows_of(up_early, 1)], 0))
    down = held(
        join(downs, 1),
        join([columns(down_early, 0), down_last, columns(down_early, 2), columns(down_early, 1)], 1),
    )
    up, down = held(join(up, 1), join(down, 0))

    near = join([first, left, right], 1)
    near_acts, near_grads = forward(near, up, down)
    *far, near_acts, near_grads = held(*far, near_acts, near_grads)
    far = join(far, 1)
    far_acts, far_grads = forward(far, up, down)

    far_sums = backward(far_acts, far_grads, up, down)
    far_back = [far_sums[:, :half], far_sums[:, half:]]
    *far_back, near_acts, near_grads, far_acts, far_grads = held(
        *far_back, near_acts, near_grads, far_acts, far_grads
    )
    far_back = [plane(far_back[0], 1, -1), plane(far_back[1], 1, 1)]
    near_sums = backward(near_acts, near_grads, up, down)
    near_acts, near_grads, near_sums = held(near_acts, near_grads, near_sums)
    sets, acts, grads = (near, far), (near_acts, far_acts), (near_grads, far_grads)
    theirs = weight_sums(sets, acts, grads, 1)
    *far_back, near_sums, down_other, up_other = held(*far_back, near_sums, *theirs)
    mine = weight_sums(sets, acts, grads, 0)

    def total(*parts):
        value = parts[0].astype(F32)
        for part in parts[1:]:
            value = value + part.astype(F32)
        return value

    here, left, right = (near_sums[:, i * rows : (i + 1) * rows] for i in range(3))
    left = join([total(left[:, :half], far_back[0]).astype(BF), left[:, half:]], 1)
    right = join([right[:, :half], total(right[:, half:], far_back[1]).astype(BF)], 1)
    near_sent = (left, right)
    left, right = plane(left, 1, -1), plane(right, 1, 1)

    def swap(blocks, round_value):
        down_sum, up_sum, _ = held(down_other[blocks], up_other[blocks], round_value)
        return across(down_sum), across(up_sum)

    down_theirs, up_theirs = swap(3, near_sent)
    down_grad = along_x(total(mine[0][1], down_theirs).astype(BF), -1)
    up_grad = along_x(total(mine[1][1], up_theirs).astype(BF), 1)
    left, right = held(left, right)

    down_theirs, up_theirs = swap(slice(0, 3), left)
    down_grad = along_x(total(mine[0][2], down_theirs[2], down_grad).astype(BF), -1)
    up_grad = along_x(total(mine[1][2], up_theirs[2], up_grad).astype(BF), 1)
    sums = total(here, left, right).astype(BF).reshape(2, 4, sub, 4 * width)
    end = total(sums[:, 0], *(plane(sums[:, hop], 0, -hop) for hop in (1, 2, 3))).astype(BF)
    end, down_grad, up_grad = held(end, down_grad, up_grad)

    down_grad = along_x(total(mine[0][3], down_theirs[1], down_grad).astype(BF), -1)
    up_grad = along_x(total(mine[1][3], up_theirs[1], up_grad).astype(BF), 1)

    out = jnp.zeros((2, rows, width), BF)
    for k in range(4):
        sent = jnp.stack([columns(end[0], turned[k]), columns(end[1], k)])
        got = along_x(sent, -k) if k else sent
        at = (x + sign * k + 4) % 4 * sub
        out = lax.dynamic_update_slice_in_dim(out, got, at, axis=1)
    down_grad = total(mine[0][0], down_theirs[0], down_grad)
    up_grad = total(mine[1][0], up_theirs[0], up_grad)
    return out[0], out[1], up_grad, down_grad


def solution(mesh):
    spec = P(("col", "depth"), "row")
    wide = P("row", ("col", "depth"))
    return jax.shard_map(
        on_device,
        mesh=mesh,
        in_specs=(spec, wide, spec, spec),
        out_specs=(spec, spec, wide, spec),
        check_vma=False,
    )
```
